32 devices in a mesh: pts: 8 (over z, y), own: 4 (over x, core).
Axes of the slice: x: 2, y: 2, z: 4, core: 2. Of those that a mesh axis runs over, the one named last changes fastest.
Arguments:
- points: bfloat16 [8192, 1536], P(('pts', 'own')), may hold values from -6 to 6
- parent_of: int32 [8192, 1], P('pts'), may hold values from 0 to 63, as said below
- owner_of: int32 [64], replicated, may hold values from 0 to 3, as said below
- child_count: int32 [64], replicated, may hold values from 16 to 64, as said below
- centroids: bfloat16 [4, 1024, 1536], P('own'), may hold values from -6 to 6
Outputs:
- new_centroids: bfloat16 [4, 1024, 1536], P('own', 'pts')
The draws below stay inside these ranges and needn't reach their ends.
Inputs may be any that keep to these rules, and one draw needn't show every extreme that they name: `owner_of`: each owner is named by exactly 16 parents. `child_count`: exactly 64 for at least one parent. `parent_of`: every parent is named by some point; in the 256 rows of one device, exactly 128 rows have parents of one owner, and all devices with the same pts index pick the same such owner; the rest of the device's rows go to the other owners as evenly as possible, so no owner gets more than 128 rows of one device.
All inputs are finite; a program needn't handle non-finite values.
Results may differ from the reference program's by a relative error of at most 0.0031.
Values may be sent and summed in bfloat16 or wider, within the bound.
No kernel may reach another device: no remote copies, remote signals or barrier semaphores. Data moves between devices by JAX's collectives and lax.ppermute only.
A program may use at most 128 MiB of HBM per device.

```python
import jax
import jax.numpy as jnp
from jax import lax

D = 1536
MC = 64
GO = 16
SWEEPS = 2
TOK_DEV = 256
KO = 1024
G = 64
POINTS = 8192


def parent_order(key):
    return jax.random.permutation(jax.random.fold_in(key, 11), G).astype(jnp.int32)


def draw_owner_of(key, part):
    order = parent_order(key)
    ranks = jnp.arange(G, dtype=jnp.int32) // GO
    return jnp.zeros((G,), jnp.int32).at[order].set(ranks)


def draw_child_count(key, part):
    counts = jax.random.randint(jax.random.fold_in(key, 23), (G,), MC // 4, MC + 1)
    where_full = jax.random.randint(jax.random.fold_in(key, 37), (), 0, G)
    return counts.at[where_full].set(MC).astype(jnp.int32)


def draw_parent_of(key, part):
    order = parent_order(key)
    owners = G // GO
    blocks = POINTS // TOK_DEV
    cap = 2 * TOK_DEV // owners
    shift = jax.random.randint(jax.random.fold_in(key, 41), (), 0, owners)
    block_ids = jnp.arange(blocks, dtype=jnp.int32)
    full_owner = (block_ids // owners + shift) % owners
    offsets = jax.random.randint(jax.random.fold_in(key, 43), (blocks,), 0, owners - 1)
    noise = jax.random.randint(jax.random.fold_in(key, 47), (blocks, TOK_DEV), 0, 1 << 20)
    scores = noise * TOK_DEV + jnp.arange(TOK_DEV, dtype=jnp.int32)[None, :]
    placed = jnp.argsort(scores, axis=1)
    rank = jnp.argsort(placed, axis=1).astype(jnp.int32)
    rest = rank - cap
    other = (full_owner[:, None] + 1 + (rest + offsets[:, None]) % (owners - 1)) % owners
    owner = jnp.where(rank < cap, full_owner[:, None], other)
    loose = jax.random.randint(jax.random.fold_in(key, 53), (blocks, TOK_DEV), 0, GO)
    within = jnp.where(rank < cap, rank % GO, loose)
    parent = order[(owner * GO + within).reshape(-1)]
    return parent.reshape(POINTS, 1).astype(jnp.int32)


def centroid_table(key):
    owners = G // GO
    sub = jax.random.fold_in(key, 61)
    values = jax.random.normal(sub, (owners, KO, D), jnp.float32)
    return jnp.clip(values, -6.0, 6.0)


def draw_centroids(key, part):
    return centroid_table(key).astype(jnp.bfloat16)


def draw_points(key, part):
    parent = draw_parent_of(key, part)[:, 0]
    owners_of = draw_owner_of(key, part)
    counts = draw_child_count(key, part)
    parent_range = jnp.arange(G, dtype=jnp.int32)
    same_owner = owners_of[:, None] == owners_of[None, :]
    earlier = parent_range[None, :] < parent_range[:, None]
    first = jnp.sum(jnp.where(same_owner & earlier, counts[None, :], 0), axis=1).astype(jnp.int32)
    row_owner = owners_of[parent]
    row_first = first[parent]
    row_count = counts[parent]
    pick_one = jax.random.randint(jax.random.fold_in(key, 71), (POINTS,), 0, row_count)
    pick_two = jax.random.randint(jax.random.fold_in(key, 73), (POINTS,), 0, row_count)
    primary = jnp.minimum(pick_one, pick_two)
    step_over = jax.random.randint(jax.random.fold_in(key, 79), (POINTS,), 0, row_count - 1)
    second = (primary + 1 + step_over) % row_count
    table = centroid_table(key).reshape(-1, D)
    base_row = row_owner * KO + row_first
    near = table[base_row + primary]
    beside = table[base_row + second]
    lead = jax.random.uniform(jax.random.fold_in(key, 83), (POINTS, 1), jnp.float32, 0.5, 0.8)
    trail = jax.random.uniform(jax.random.fold_in(key, 89), (POINTS, 1), jnp.float32, 0.3, 0.6)
    noise = jax.random.normal(jax.random.fold_in(key, 97), (POINTS, D), jnp.float32)
    values = lead * near + trail * beside + noise
    return jnp.clip(values, -6.0, 6.0).astype(jnp.bfloat16)


def setup_inputs(seed: int = 0) -> dict:
    splits = jax.random.split(jax.random.key(seed), 6)
    return {
        "points": draw_points(jax.random.fold_in(splits[5], 71), 0),
        "parent_of": draw_parent_of(jax.random.fold_in(splits[5], 71), 0),
        "owner_of": draw_owner_of(jax.random.fold_in(splits[5], 71), 0),
        "child_count": draw_child_count(jax.random.fold_in(splits[5], 71), 0),
        "centroids": draw_centroids(jax.random.fold_in(splits[5], 71), 0),
    }


def unit_rms(values):
    values = values.astype(jnp.float32)
    return values * lax.rsqrt(lax.optimization_barrier(jnp.mean(values * values, axis=-1, keepdims=True)) + 1e-06)

def reference(points, parent_of, owner_of, child_count, centroids):
    width = points.shape[1]
    point_unit = unit_rms(points).astype(jnp.bfloat16)
    parent_ids = parent_of[:, 0]
    parent_range = jnp.arange(owner_of.shape[0], dtype=jnp.int32)
    same_owner = owner_of[:, None] == owner_of[None, :]
    earlier = parent_range[None, :] < parent_range[:, None]
    first_slot = lax.optimization_barrier(jnp.sum(jnp.where(same_owner & earlier, child_count[None, :], 0), axis=1)).astype(jnp.int32)
    row_owner = owner_of[parent_ids]
    row_first = first_slot[parent_ids]
    row_count = child_count[parent_ids]
    slot_index = jnp.arange(KO, dtype=jnp.int32)

    def per_owner(owner):
        cent_unit = unit_rms(centroids[owner]).astype(jnp.bfloat16)
        in_range = (row_owner == owner)[:, None] & (slot_index[None, :] >= row_first[:, None]) & (slot_index[None, :] < (row_first + row_count)[:, None])
        table_range = (owner_of == owner)[:, None] & (slot_index[None, :] >= first_slot[:, None]) & (slot_index[None, :] < (first_slot + child_count)[:, None])
        slot_used = jnp.any(table_range, axis=0)
        row_live = row_owner == owner
        scores = jnp.dot(point_unit, cent_unit.T, preferred_element_type=jnp.float32) / (width * 0.05)
        weights = jnp.where(in_range, jnp.exp(scores), jnp.float32(0.0))
        for sweep in range(SWEEPS):
            column_sum = lax.optimization_barrier(jnp.sum(weights, axis=0))
            weights = weights / jnp.where(slot_used, column_sum, jnp.float32(1.0))[None, :]
            row_sum = lax.optimization_barrier(jnp.sum(weights, axis=1))
            weights = weights / jnp.where(row_live, row_sum, jnp.float32(1.0))[:, None]
        assign = weights.astype(jnp.bfloat16)
        moved = jnp.dot(assign.T, point_unit, preferred_element_type=jnp.float32)
        return unit_rms(cent_unit.astype(jnp.float32) + 8.0 * moved).astype(jnp.bfloat16)
    return lax.map(per_owner, jnp.arange(centroids.shape[0], dtype=jnp.int32))
```

```python
import functools

import jax
import jax.numpy as jnp
from jax import lax
from jax.experimental import pallas as pl
from jax.experimental.pallas import tpu as pltpu
from jax.sharding import PartitionSpec as P

F32 = jnp.float32
BF16 = jnp.bfloat16
I32 = jnp.int32
CORES = 2
ROWS = 16
LANES = 128
VMEM_LIMIT = 40 * 1024 * 1024
OWNER_SHIFT = 1 << 17
FIRST_SHIFT = 1 << 7


def down(value):
    return value // ROWS * ROWS


def up(value):
    return -(-value // ROWS) * ROWS


def iota(shape, dim):
    return lax.broadcasted_iota(I32, shape, dim)


def unit_rms(values):
    values = values.astype(F32)
    return values * lax.rsqrt(jnp.mean(values * values, axis=-1, keepdims=True) + 1e-06)


def windows(tok, owners):
    chips = owners // CORES
    full = 2 * tok // owners
    least = CORES * ((tok - full) // max(owners - 1, 1))
    starts = [down(j * least) for j in range(chips)]
    ends = [up(tok - (chips - 1 - j) * least) for j in range(chips)]
    wide = max(e - s for s, e in zip(starts, ends))
    return [min(s, tok - wide) for s in starts], wide


def to_col(row):
    n = row.shape[1]
    return jnp.sum(jnp.where(iota((n, n), 0) == iota((n, n), 1), row, 0.0), axis=1, keepdims=True)


def to_row(col):
    n = col.shape[0]
    return jnp.sum(jnp.where(iota((n, n), 0) == iota((n, n), 1), col, 0.0), axis=0, keepdims=True)


def owner_codes(owner_ref, count_ref):
    owner = owner_ref[...].astype(F32)
    count = count_ref[...].astype(F32)
    n = owner.shape[1]
    earlier = (to_col(owner) == owner) & (iota((n, n), 0) < iota((n, n), 1))
    first = jnp.sum(jnp.where(earlier, to_col(count), 0.0), axis=0, keepdims=True)
    return owner * OWNER_SHIFT + first * FIRST_SHIFT + count


def code_and_key(parent_row, code_row, chip, chips):
    parent = to_col(parent_row.astype(F32)).astype(I32)
    tok = parent.shape[0]
    n = code_row.shape[1]
    code = jnp.sum(jnp.where(parent == iota((tok, n), 1), code_row, 0.0), axis=1, keepdims=True)
    owner = code.astype(I32) // OWNER_SHIFT
    order = (chips - 1) - ((owner // CORES) ^ chip)
    key = (order * tok + iota((tok, 1), 0)).astype(F32)
    return code, key


def sort_kernel(chips, points_ref, parents_ref, owner_ref, count_ref, out_ref):
    me = lax.axis_index("own")
    code_row = owner_codes(owner_ref, count_ref)
    parent = parents_ref[pl.ds(me, 1), :]
    code, key = code_and_key(parent, code_row, me // CORES, chips)
    tok = key.shape[0]
    key_row = to_row(key)
    place = jnp.sum(jnp.where(key < key_row, 1.0, 0.0), axis=0, keepdims=True).astype(I32)
    pick = jnp.where(iota((tok, tok), 0) == place, 1.0, 0.0).astype(BF16)
    unit = unit_rms(points_ref[...]).astype(BF16)
    out_ref[...] = jnp.dot(pick, unit, preferred_element_type=F32).astype(BF16)


def codes_kernel(chips, starts, parents_ref, owner_ref, count_ref, out_ref):
    me = lax.axis_index("own")
    code_row = owner_codes(owner_ref, count_ref)
    wide = out_ref.shape[1]
    for rel in range(out_ref.shape[0]):
        parent = parents_ref[pl.ds(me ^ rel, 1), :]
        code, key = code_and_key(parent, code_row, (me ^ rel) // CORES, chips)
        tok = key.shape[0]
        place = jnp.sum(jnp.where(to_row(key) < key, 1.0, 0.0), axis=1, keepdims=True).astype(I32)
        start = starts[chips - 1 - rel // CORES]
        hit = place == iota((tok, wide), 1) + start
        out_ref[rel : rel + 1, :] = jnp.sum(jnp.where(hit, code, 0.0), axis=0, keepdims=True)


def cent_kernel(in_ref, out_ref):
    out_ref[...] = unit_rms(in_ref[...]).astype(BF16)


def weights_kernel(rels, tile, *refs):
    n = len(rels)
    row_refs, (codes_ref, cent_ref, w_ref, sum_ref, rows_ref, low_ref, high_ref) = refs[:n], refs[n:]
    me = lax.axis_index("own")
    wide, width = row_refs[0].shape
    slots = cent_ref.shape[0]
    for k, rel in enumerate(rels):
        part = slice(k * wide, (k + 1) * wide)
        rows_ref[part, :] = row_refs[k][...]
        code = to_col(codes_ref[rel : rel + 1, :]).astype(I32)
        first = (code % OWNER_SHIFT) // FIRST_SHIFT
        low = jnp.where(code // OWNER_SHIFT == me, first, slots)
        low_ref[part, :] = low
        high_ref[part, :] = low + code % FIRST_SHIFT

    def step(i, carry):
        at = pl.multiple_of(i * tile, tile)
        cent = cent_ref[pl.ds(at, tile), :]
        scores = lax.dot_general(rows_ref[...], cent, (((1,), (1,)), ((), ())), preferred_element_type=F32)
        slot = iota(scores.shape, 1) + at
        live = (slot >= low_ref[...]) & (slot < high_ref[...])
        w = jnp.where(live, jnp.exp(scores * (1.0 / (width * 0.05))), 0.0)
        w_ref[:, pl.ds(at, tile)] = w
        sum_ref[:, pl.ds(at, tile)] = jnp.sum(w, axis=0, keepdims=True)
        return carry

    lax.fori_loop(0, slots // tile, step, 0)


def inverse(values):
    return jnp.where(values > 0.0, 1.0 / jnp.where(values > 0.0, values, 1.0), 0.0)


def balance_kernel(n, *refs):
    w_refs, col_ref, out_ref = refs[:n], refs[n], refs[n + 1]
    scale = inverse(col_ref[...])
    total = jnp.zeros_like(scale)
    for w_ref in w_refs:
        rows = w_ref.shape[0]
        for at in range(0, rows, ROWS * 2):
            w = w_ref[at : at + ROWS * 2, :]
            row = jnp.sum(w * scale, axis=1, keepdims=True)
            total = total + jnp.sum(w * inverse(row), axis=0, keepdims=True)
    out_ref[...] = total


def move_kernel(nw, nr, routes, cols, half_bit, low_mask, *refs):
    w_refs, row_refs, t_ref = refs[:nw], refs[nw : nw + nr], refs[nw + nr]
    rest = refs[nw + nr + 1 :]
    keep_refs, send_refs = rest[: len(routes)], rest[len(routes) : 2 * len(routes)]
    assign_ref, rows_ref, part_ref = rest[2 * len(routes) :]
    p = lax.axis_index("pts")
    scale = inverse(t_ref[...])
    half = assign_ref.shape[1]
    upper = (p // half_bit) % 2
    at = 0
    for w_ref in w_refs:
        rows = w_ref.shape[0]
        for lo in range(0, rows, ROWS * 2):
            w = w_ref[lo : lo + ROWS * 2, :] * scale
            row = inverse(jnp.sum(w, axis=1, keepdims=True))
            mine = jnp.where(upper == 0, w[:, :half], w[:, half:])
            assign_ref[at : at + ROWS * 2, :] = (mine * row).astype(BF16)
            at += ROWS * 2
    at = 0
    for r in row_refs:
        rows_ref[at : at + r.shape[0], :] = r[...]
        at += r.shape[0]
    low = p % half_bit
    share = half // half_bit
    for which, order in enumerate(routes):
        lanes = slice(which * cols, (which + 1) * cols)
        m = keep_refs[which].shape[0]

        for k, rel in enumerate(order):
            start = (low ^ rel) * share
            block = part_ref.shape[0]
            a = assign_ref[:, pl.ds(pl.multiple_of(start // block * block, block), block)]
            moved = lax.dot_general(
                a, rows_ref[:, lanes], (((0,), (0,)), ((), ())), preferred_element_type=F32
            )
            if share < block:
                part_ref[...] = moved
                moved = part_ref[pl.ds(pl.multiple_of(start % block, share), share), :]
            if k < m:
                keep_refs[which][k] = moved
            else:
                send_refs[which][k - m] = moved.astype(BF16)


def final_kernel(nroute, nterm, *refs):
    base_ref, out_ref = refs[nroute * nterm], refs[nroute * nterm + 1]
    parts = []
    for which in range(nroute):
        total = refs[which * nterm][...].astype(F32)
        for k in range(1, nterm):
            total = total + refs[which * nterm + k][...].astype(F32)
        parts.append(total)
    moved = jnp.concatenate(parts, axis=1)
    out_ref[...] = unit_rms(base_ref[...].astype(F32) + 8.0 * moved).astype(BF16)


def call(kernel, outs, *args, scratch=(), flops=0):
    shapes = [jax.ShapeDtypeStruct(s, d) for s, d in outs]
    size = sum(a.size * a.dtype.itemsize for a in args) + sum(s.size * s.dtype.itemsize for s in shapes)
    got = pl.pallas_call(
        kernel,
        out_shape=shapes,
        in_specs=[pl.BlockSpec(memory_space=pltpu.VMEM)] * len(args),
        out_specs=[pl.BlockSpec(memory_space=pltpu.VMEM)] * len(shapes),
        scratch_shapes=list(scratch),
        compiler_params=pltpu.CompilerParams(vmem_limit_bytes=VMEM_LIMIT),
        cost_estimate=pl.CostEstimate(flops=flops, bytes_accessed=size, transcendentals=0),
    )(*args)
    return got[0] if len(shapes) == 1 else got


def swap(values, axis, bit):
    return lax.ppermute(values, axis, [(i, i ^ bit) for i in range(lax.axis_size(axis))])


def bit_orders(bits):
    orders = []
    for k in range(len(bits)):
        order = bits[k:] + bits[:k]
        blocks = [0]
        for bit in reversed(order):
            blocks = blocks + [b | bit for b in blocks]
        orders.append((order, blocks))
    return orders


def local(points, parent_of, owner_of, child_count, centroids):
    owners, groups = lax.axis_size("own"), lax.axis_size("pts")
    chips = owners // CORES
    tok, width = points.shape
    slots = centroids.shape[1]
    share = slots // groups
    starts, wide = windows(tok, owners)
    parents = parent_of.reshape(owners, tok)
    owner_row = owner_of.reshape(1, -1)
    count_row = child_count.reshape(1, -1)
    half_bit = groups // 2

    ordered = call(
        functools.partial(sort_kernel, chips), [((tok, width), BF16)], points, parents, owner_row, count_row,
        flops=2 * tok * tok * width,
    )
    outward = starts[max(chips - 2, 0)] + wide

    def spread(head, tail):
        blocks = {}
        for chip in range(1, chips):
            start = starts[chips - 1 - chip]
            blocks[chip * CORES] = swap(head[start : start + wide], "own", chip * CORES)
        start = starts[chips - 1]
        blocks[0] = jnp.concatenate([head[start:], tail], axis=0)
        for chip in range(chips):
            blocks[chip * CORES + 1] = swap(blocks[chip * CORES], "own", 1)
        return blocks

    head, tail = ordered[:outward], ordered[outward:]
    near = spread(head, tail)
    far_head, far_tail = swap(head, "pts", half_bit), swap(tail, "pts", half_bit)
    far = spread(far_head, far_tail)
    codes = call(
        functools.partial(codes_kernel, chips, starts), [((owners, wide), F32)], parents, owner_row, count_row
    )
    far_codes = swap(codes, "pts", half_bit)
    cent = call(cent_kernel, [((slots, width), BF16)], centroids[0])

    def weigh(blocks, codes, rels):
        rows = wide * len(rels)
        return call(
            functools.partial(weights_kernel, rels, min(slots, 256)),
            [((rows, slots), F32), ((1, slots), F32)],
            *[blocks[r] for r in rels], codes, cent,
            scratch=[pltpu.VMEM((rows, width), BF16), pltpu.VMEM((rows, 1), I32), pltpu.VMEM((rows, 1), I32)],
            flops=2 * rows * width * slots,
        )

    def all_sum(values):
        bit = 1
        while bit < groups:
            values = values + swap(values, "pts", bit)
            bit *= 2
        return values

    pairs = [list(range(c * CORES, (c + 1) * CORES)) for c in range(chips)]
    near_w, far_w, partial = [], [], None
    for rels in pairs:
        w, s = weigh(near, codes, rels)
        near_w.append(w)
        partial = s if partial is None else partial + s
    for rels in pairs:
        far_w.append(weigh(far, far_codes, rels)[0])
    column = all_sum(partial)
    balance = all_sum(call(functools.partial(balance_kernel, chips), [((1, slots), F32)], *near_w, column))

    bits = []
    bit = 1
    while bit < half_bit:
        bits.append(bit)
        bit *= 2
    orders = bit_orders(bits)
    cols = width // len(orders)
    m = half_bit // 2
    rows = [near[r] for r in range(owners)] + [far[r] for r in range(owners)]
    total_rows = wide * len(rows)
    got = call(
        functools.partial(
            move_kernel, 2 * chips, len(rows), [b for _, b in orders], cols, half_bit, half_bit - 1
        ),
        [((m, share, cols), F32)] * len(orders) + [((m, share, cols), BF16)] * len(orders),
        *near_w, *far_w, *rows, balance,
        scratch=[pltpu.VMEM((total_rows, slots // 2), BF16), pltpu.VMEM((total_rows, width), BF16),
                 pltpu.VMEM((max(share, LANES), cols), F32)],
        flops=2 * total_rows * width * slots // 2,
    )
    keeps, sends = got[: len(orders)], got[len(orders) :]
    terms = [[k] for k in keeps]
    for step in range(len(bits)):
        arrived = [swap(s, "pts", orders[r][0][step]) for r, s in enumerate(sends)]
        sends = []
        for r, a in enumerate(arrived):
            terms[r].append(a)
            n = a.shape[0] // 2
            if n:
                sends.append(sum(t[n:].astype(F32) for t in terms[r]).astype(BF16))
                terms[r] = [t[:n] for t in terms[r]]
    own = lax.axis_index("pts") * share
    base = lax.dynamic_slice_in_dim(cent, own, share, 0)
    flat = [t.reshape(share, cols) for route in terms for t in route]
    out = call(
        functools.partial(final_kernel, len(orders), len(bits) + 1), [((share, width), BF16)], *flat, base
    )
    return out[None]


def solution(mesh):
    in_specs = (P(("pts", "own"), None), P("pts", None), P(), P(), P("own", None, None))
    out_specs = P("own", "pts", None)
    return jax.shard_map(local, mesh=mesh, in_specs=in_specs, out_specs=out_specs, check_vma=False)
```

```python
import functools

import jax
import jax.numpy as jnp
from jax import lax
from jax.experimental import pallas as pl
from jax.experimental.pallas import tpu as pltpu
from jax.sharding import PartitionSpec as P

F32 = jnp.float32
BF16 = jnp.bfloat16
I32 = jnp.int32
CORES = 2
ROWS = 16
LANES = 128
OWNER_SHIFT = 1 << 17
FIRST_SHIFT = 1 << 7


def down(value):
    return value // ROWS * ROWS


def up(value):
    return -(-value // ROWS) * ROWS


def iota(shape, dim):
    return lax.broadcasted_iota(I32, shape, dim)


def unit_rms(values):
    values = values.astype(F32)
    return values * lax.rsqrt(jnp.mean(values * values, axis=-1, keepdims=True) + 1e-06)


def windows(tok, owners):
    chips = owners // CORES
    full = 2 * tok // owners
    least = CORES * ((tok - full) // max(owners - 1, 1))
    starts = [down(j * least) for j in range(chips)]
    ends = [up(tok - (chips - 1 - j) * least) for j in range(chips)]
    wide = max(e - s for s, e in zip(starts, ends))
    starts = [min(s, tok - wide) for s in starts]
    return starts, wide


def to_col(row):
    n = row.shape[1]
    return jnp.sum(jnp.where(iota((n, n), 0) == iota((n, n), 1), row, 0.0), axis=1, keepdims=True)


def to_row(col):
    n = col.shape[0]
    return jnp.sum(jnp.where(iota((n, n), 0) == iota((n, n), 1), col, 0.0), axis=0, keepdims=True)


def owner_codes(owner_ref, count_ref):
    owner = owner_ref[...].astype(F32)
    count = count_ref[...].astype(F32)
    n = owner.shape[1]
    earlier = (to_col(owner) == owner) & (iota((n, n), 0) < iota((n, n), 1))
    first = jnp.sum(jnp.where(earlier, to_col(count), 0.0), axis=0, keepdims=True)
    return owner * OWNER_SHIFT + first * FIRST_SHIFT + count


def code_and_key(parent_row, code_row, chip, chips):
    parent = to_col(parent_row.astype(F32)).astype(I32)
    tok = parent.shape[0]
    n = code_row.shape[1]
    code = jnp.sum(jnp.where(parent == iota((tok, n), 1), code_row, 0.0), axis=1, keepdims=True)
    owner = code.astype(I32) // OWNER_SHIFT
    order = (chips - 1) - ((owner // CORES) ^ chip)
    key = (order * tok + iota((tok, 1), 0)).astype(F32)
    return code, key


def fetch(pairs, sems):
    copies = [pltpu.make_async_copy(src, dst, sems.at[k]) for k, (src, dst) in enumerate(pairs)]
    for copy in copies:
        copy.start()
    return copies


def sort_kernel(chips, ranges, *refs):
    points_ref, parents_ref, owner_ref, count_ref = refs[:4]
    out_refs, (points, parents, owner, count, sems) = refs[4:-5], refs[-5:]
    copies = fetch(
        [(points_ref, points), (parents_ref, parents), (owner_ref, owner), (count_ref, count)], sems
    )
    me = lax.axis_index("own")
    tok = points.shape[0]
    for copy in copies[1:]:
        copy.wait()
    code_row = owner_codes(owner, count)
    parent = parents[:, pl.ds(pl.multiple_of(me * tok, tok), tok)]
    code, key = code_and_key(parent, code_row, me // CORES, chips)
    key_row = to_row(key)
    place = jnp.sum(jnp.where(key < key_row, 1.0, 0.0), axis=0, keepdims=True).astype(I32)
    pick = jnp.where(iota((tok, tok), 0) == place, 1.0, 0.0).astype(BF16)
    copies[0].wait()
    unit = unit_rms(points[...]).astype(BF16)
    ordered = jnp.dot(pick, unit, preferred_element_type=F32).astype(BF16)
    for (lo, hi), out_ref in zip(ranges, out_refs):
        out_ref[...] = ordered[lo:hi]


def codes_kernel(chips, starts, tok, parents_ref, owner_ref, count_ref, out_ref, parents, owner, count, sems):
    for copy in fetch([(parents_ref, parents), (owner_ref, owner), (count_ref, count)], sems):
        copy.wait()
    me = lax.axis_index("own")
    code_row = owner_codes(owner, count)
    wide = out_ref.shape[1]
    for rel in range(out_ref.shape[0]):
        parent = parents[:, pl.ds(pl.multiple_of((me ^ rel) * tok, tok), tok)]
        code, key = code_and_key(parent, code_row, (me ^ rel) // CORES, chips)
        place = jnp.sum(jnp.where(to_row(key) < key, 1.0, 0.0), axis=1, keepdims=True).astype(I32)
        start = starts[chips - 1 - rel // CORES]
        hit = place == iota((tok, wide), 1) + start
        out_ref[rel : rel + 1, :] = jnp.sum(jnp.where(hit, code, 0.0), axis=0, keepdims=True)


def cent_kernel(in_ref, out_ref):
    out_ref[...] = unit_rms(in_ref[...]).astype(BF16)


def weights_kernel(rels, tile, skips, *refs):
    row_refs, (codes_ref, cent_ref, w_ref, sum_ref, rows_ref, low_ref, high_ref) = refs[:-7], refs[-7:]
    me = lax.axis_index("own")
    slots, width = cent_ref.shape
    wide = codes_ref.shape[1]
    at = 0
    for row_ref, skip in zip(row_refs, skips):
        size = row_ref.shape[0] - skip
        rows_ref[at : at + size, :] = row_ref[skip:, :]
        at += size
    for k, rel in enumerate(rels):
        part = slice(k * wide, (k + 1) * wide)
        code = to_col(codes_ref[rel : rel + 1, :]).astype(I32)
        first = (code % OWNER_SHIFT) // FIRST_SHIFT
        low = jnp.where(code // OWNER_SHIFT == me, first, slots)
        low_ref[part, :] = low
        high_ref[part, :] = low + code % FIRST_SHIFT

    def step(i, carry):
        at = pl.multiple_of(i * tile, tile)
        cent = cent_ref[pl.ds(at, tile), :]
        scores = lax.dot_general(rows_ref[...], cent, (((1,), (1,)), ((), ())), preferred_element_type=F32)
        slot = iota(scores.shape, 1) + at
        live = (slot >= low_ref[...]) & (slot < high_ref[...])
        w = jnp.where(live, jnp.exp(scores * (1.0 / (width * 0.05))), 0.0)
        w_ref[:, pl.ds(at, tile)] = w
        sum_ref[:, pl.ds(at, tile)] = jnp.sum(w, axis=0, keepdims=True)
        return carry

    lax.fori_loop(0, slots // tile, step, 0)


def inverse(values):
    return jnp.where(values > 0.0, 1.0 / jnp.where(values > 0.0, values, 1.0), 0.0)


def balance_kernel(n, *refs):
    w_refs, col_ref, out_ref = refs[:n], refs[n], refs[n + 1]
    scale = inverse(col_ref[...])
    total = jnp.zeros_like(scale)
    for w_ref in w_refs:
        rows = w_ref.shape[0]
        for at in range(0, rows, ROWS * 2):
            w = w_ref[at : at + ROWS * 2, :]
            row = jnp.sum(w * scale, axis=1, keepdims=True)
            total = total + jnp.sum(w * inverse(row), axis=0, keepdims=True)
    out_ref[...] = total


def assign_kernel(half_bit, *refs):
    w_refs, (t_ref, assign_ref) = refs[:-2], refs[-2:]
    scale = inverse(t_ref[...])
    half = assign_ref.shape[1]
    upper = (lax.axis_index("pts") // half_bit) % 2
    at = 0
    for w_ref in w_refs:
        for lo in range(0, w_ref.shape[0], ROWS * 2):
            w = w_ref[lo : lo + ROWS * 2, :] * scale
            row = inverse(jnp.sum(w, axis=1, keepdims=True))
            mine = jnp.where(upper == 0, w[:, :half], w[:, half:])
            assign_ref[at : at + ROWS * 2, :] = (mine * row).astype(BF16)
            at += ROWS * 2


def move_kernel(routes, half_bit, assign_ref, row_refs, out_refs, part_ref):
    low = lax.axis_index("pts") % half_bit
    for which, (order, out_ref) in enumerate(zip(routes, out_refs)):
        share, cols = out_ref.shape[1:]
        block = part_ref.shape[0]
        lanes = slice(which * cols, (which + 1) * cols)
        for k, rel in enumerate(order):
            start = (low ^ rel) * share
            columns = pl.ds(pl.multiple_of(start // block * block, block), block)
            moved, at = 0.0, 0
            for r in row_refs:
                a = assign_ref[at : at + r.shape[0], columns]
                moved = moved + lax.dot_general(
                    a, r[:, lanes], (((0,), (0,)), ((), ())), preferred_element_type=F32
                )
                at += r.shape[0]
            if share < block:
                part_ref[...] = moved
                moved = part_ref[pl.ds(pl.multiple_of(start % block, share), share), :]
            out_ref[k] = moved.astype(out_ref.dtype)


def send_kernel(routes, half_bit, nw, *refs):
    n = len(routes)
    row_refs, out_refs = refs[nw + 1 : -n - 2], refs[-n - 2 : -2]
    assign_ref, part_ref = refs[-2:]
    assign_kernel(half_bit, *refs[: nw + 1], assign_ref)
    move_kernel(routes, half_bit, assign_ref, row_refs, out_refs, part_ref)


def keep_kernel(routes, half_bit, *refs):
    n = len(routes)
    move_kernel(routes, half_bit, refs[0], refs[1 : -n - 1], refs[-n - 1 : -1], refs[-1])


def merge_kernel(keep_ref, came_ref, *out_refs):
    total = keep_ref[...] + came_ref[...].astype(F32)
    n = total.shape[0] // 2
    out_refs[0][...] = total[:n]
    out_refs[1][...] = total[n:].astype(BF16)


def final_kernel(nroute, nterm, *refs):
    base_ref, out_ref = refs[nroute * nterm], refs[nroute * nterm + 1]
    parts = []
    for which in range(nroute):
        total = refs[which * nterm][...].astype(F32)
        for k in range(1, nterm):
            total = total + refs[which * nterm + k][...].astype(F32)
        parts.append(total)
    moved = jnp.concatenate(parts, axis=1)
    out_ref[...] = unit_rms(base_ref[...].astype(F32) + 8.0 * moved).astype(BF16)


def call(kernel, outs, *args, scratch=(), vmem=16, where=pltpu.VMEM):
    shapes = [jax.ShapeDtypeStruct(s, d) for s, d in outs]
    size = sum(a.size * a.dtype.itemsize for a in args) + sum(s.size * s.dtype.itemsize for s in shapes)
    got = pl.pallas_call(
        kernel,
        out_shape=shapes,
        in_specs=[pl.BlockSpec(memory_space=where)] * len(args),
        out_specs=[pl.BlockSpec(memory_space=pltpu.VMEM)] * len(shapes),
        scratch_shapes=list(scratch),
        compiler_params=pltpu.CompilerParams(vmem_limit_bytes=vmem << 20),
        cost_estimate=pl.CostEstimate(flops=0, bytes_accessed=0, transcendentals=0),
    )(*args)
    return got[0] if len(shapes) == 1 else got


def after(values, gate):
    return lax.optimization_barrier((values, gate))[0]


def swap(values, axis, bit):
    return lax.ppermute(values, axis, [(i, i ^ bit) for i in range(lax.axis_size(axis))])


def bit_orders(bits):
    orders = []
    for k in range(len(bits)):
        order = bits[k:] + bits[:k]
        blocks = [0]
        for bit in reversed(order):
            blocks = blocks + [b | bit for b in blocks]
        orders.append((order, blocks))
    return orders


def local(points, parent_of, owner_of, child_count, centroids):
    owners, groups = lax.axis_size("own"), lax.axis_size("pts")
    chips = owners // CORES
    tok, width = points.shape
    slots = centroids.shape[1]
    share = slots // groups
    starts, wide = windows(tok, owners)
    parents = parent_of.T
    table = [owner_of.reshape(1, -1), child_count.reshape(1, -1)]
    half_bit = groups // 2
    small = [pltpu.VMEM(a.shape, I32) for a in [parents, *table]]
    own_start, outward = starts[-1], starts[max(chips - 2, 0)] + wide

    ranges = [(0, outward), (outward, tok), (own_start, tok)]
    head, tail, mine = call(
        functools.partial(sort_kernel, chips, ranges), [((hi - lo, width), BF16) for lo, hi in ranges],
        points, parents, *table,
        scratch=[pltpu.VMEM((tok, width), BF16), *small, pltpu.SemaphoreType.DMA((4,))], where=pl.ANY, vmem=62,
    )

    def across(held, chip):
        start = starts[chips - 1 - chip]
        whole = start == 0 and start + wide == held.shape[0]
        return swap(held if whole else held[start : start + wide], "own", chip * CORES)

    def both(rows):
        return [*rows, *[swap(r, "own", 1) for r in rows]]

    def weigh(blocks, codes, chip, skip):
        rows = wide * CORES
        skips = [skip, 0] * CORES if skip else [0] * len(blocks)
        return call(
            functools.partial(weights_kernel, [chip * CORES, chip * CORES + 1], min(slots, 256), skips),
            [((rows, slots), F32), ((1, slots), F32), ((rows, width), BF16)],
            *blocks, codes, cent,
            scratch=[pltpu.VMEM((rows, 1), I32), pltpu.VMEM((rows, 1), I32)],
        )

    def all_sum(values):
        seen = [values]
        bit = 1
        while bit < groups:
            values = values + swap(values, "pts", bit)
            seen.append(values)
            bit *= 2
        return values, seen

    near = [both([mine])] + [both([across(head, chip)]) for chip in range(1, chips)]
    far_head, far_tail = swap(head, "pts", half_bit), swap(tail, "pts", half_bit)
    codes = call(
        functools.partial(codes_kernel, chips, starts, tok), [((owners, wide), F32)], parents, *table,
        scratch=[*small, pltpu.SemaphoreType.DMA((3,))], where=pl.ANY,
    )
    far_codes = swap(codes, "pts", half_bit)
    cent = call(cent_kernel, [((slots, width), BF16)], centroids[0])

    near_got = [
        weigh(near[chip], codes if chip == 0 else after(codes, far_codes), chip, 0) for chip in range(chips)
    ]
    near_w, near_s, near_x = zip(*near_got)
    column, seen = all_sum(sum(near_s))
    balance, then = all_sum(
        call(functools.partial(balance_kernel, chips), [((1, slots), F32)], *near_w, column)
    )
    far_cross = [across(after(far_head, seen[0]), chip) for chip in range(1, chips)]
    far = [both([after(far_head, column), after(far_tail, column)])] + [both([after(r, then[1])]) for r in far_cross]
    far_got = [
        weigh(far[chip], after(far_codes, then[1] if chip == 0 else then[-2]), chip, own_start if chip == 0 else 0)
        for chip in range(chips)
    ]
    far_w, _, far_x = zip(*far_got)

    bits = []
    bit = 1
    while bit < half_bit:
        bits.append(bit)
        bit *= 2
    orders = bit_orders(bits)
    cols = width // len(orders)
    m = half_bit // 2
    rows = [*near_x, *far_x]
    total_rows = sum(r.shape[0] for r in rows)
    part = pltpu.VMEM((max(share, LANES), cols), F32)
    got = call(
        functools.partial(send_kernel, [b[m:] for _, b in orders], half_bit, 2 * chips),
        [((m, share, cols), BF16)] * len(orders) + [((total_rows, slots // 2), BF16)],
        *near_w, *far_w, balance, *rows, scratch=[part],
    )
    sends, assign = got[:-1], got[-1]
    keeps = call(
        functools.partial(keep_kernel, [b[:m] for _, b in orders], half_bit),
        [((m, share, cols), F32)] * len(orders), assign, *rows, scratch=[part],
    )
    keeps = list(keeps) if len(orders) > 1 else [keeps]
    last = []
    for step in range(len(bits)):
        came = [swap(s, "pts", orders[r][0][step]) for r, s in enumerate(sends)]
        n = came[0].shape[0] // 2
        if n == 0:
            last = came
            break
        sends = []
        for r, c in enumerate(came):
            keeps[r], send = call(
                merge_kernel, [((n, share, cols), F32), ((n, share, cols), BF16)], keeps[r], c, vmem=8
            )
            sends.append(send)
    own = lax.axis_index("pts") * share
    base = lax.dynamic_slice_in_dim(cent, own, share, 0)
    flat = [t.reshape(share, cols) for pair in zip(keeps, last) for t in pair]
    out = call(
        functools.partial(final_kernel, len(orders), 2), [((share, width), BF16)], *flat, base, vmem=8
    )
    return out[None]


def solution(mesh):
    in_specs = (P(("pts", "own"), None), P("pts", None), P(), P(), P("own", None, None))
    out_specs = P("own", "pts", None)
    return jax.shard_map(local, mesh=mesh, in_specs=in_specs, out_specs=out_specs, check_vma=False)
```

```python
import functools

import jax
import jax.numpy as jnp
from jax import lax
from jax.experimental import pallas as pl
from jax.experimental.pallas import tpu as pltpu
from jax.sharding import PartitionSpec as P

F32 = jnp.float32
BF16 = jnp.bfloat16
I32 = jnp.int32
CORES = 2
ROWS = 16
LANES = 128
OWNER_SHIFT = 1 << 17
FIRST_SHIFT = 1 << 7


def down(value):
    return value // ROWS * ROWS


def up(value):
    return -(-value // ROWS) * ROWS


def iota(shape, dim):
    return lax.broadcasted_iota(I32, shape, dim)


def unit_rms(values):
    values = values.astype(F32)
    return values * lax.rsqrt(jnp.mean(values * values, axis=-1, keepdims=True) + 1e-06)


def windows(tok, owners):
    chips = owners // CORES
    full = 2 * tok // owners
    least = CORES * ((tok - full) // max(owners - 1, 1))
    starts = [down(j * least) for j in range(chips)]
    ends = [up(tok - (chips - 1 - j) * least) for j in range(chips)]
    wide = max(e - s for s, e in zip(starts, ends))
    starts = [min(s, tok - wide) for s in starts]
    starts = [min(s, tok - wide) for s in starts]
    cuts = sorted(set(starts + [s + wide for s in starts] + [0, tok]))
    pieces = list(zip(cuts[:-1], cuts[1:]))
    parts = [[k for k, (lo, hi) in enumerate(pieces) if s <= lo and hi <= s + wide] for s in starts]
    return starts, wide, pieces, parts


def to_col(row):
    n = row.shape[1]
    return jnp.sum(jnp.where(iota((n, n), 0) == iota((n, n), 1), row, 0.0), axis=1, keepdims=True)


def to_row(col):
    n = col.shape[0]
    return jnp.sum(jnp.where(iota((n, n), 0) == iota((n, n), 1), col, 0.0), axis=0, keepdims=True)


def owner_codes(owner_ref, count_ref):
    owner = owner_ref[...].astype(F32)
    count = count_ref[...].astype(F32)
    n = owner.shape[1]
    earlier = (to_col(owner) == owner) & (iota((n, n), 0) < iota((n, n), 1))
    first = jnp.sum(jnp.where(earlier, to_col(count), 0.0), axis=0, keepdims=True)
    return owner * OWNER_SHIFT + first * FIRST_SHIFT + count


def code_and_key(parent_row, code_row, chip, chips):
    parent = to_col(parent_row.astype(F32)).astype(I32)
    tok = parent.shape[0]
    n = code_row.shape[1]
    code = jnp.sum(jnp.where(parent == iota((tok, n), 1), code_row, 0.0), axis=1, keepdims=True)
    owner = code.astype(I32) // OWNER_SHIFT
    order = (chips - 1) - ((owner // CORES) ^ chip)
    key = (order * tok + iota((tok, 1), 0)).astype(F32)
    return code, key


def fetch(pairs, sems):
    copies = [pltpu.make_async_copy(src, dst, sems.at[k]) for k, (src, dst) in enumerate(pairs)]
    for copy in copies:
        copy.start()
    return copies


def sort_kernel(chips, ranges, *refs):
    points_ref, parents_ref, owner_ref, count_ref = refs[:4]
    out_refs, (parents, table, points, owner, count, sems) = refs[4:-6], refs[-6:]
    copies = fetch(
        [(points_ref, points), (parents_ref, parents), (owner_ref, owner), (count_ref, count)], sems
    )
    me = lax.axis_index("own")
    tok = points.shape[0]
    for copy in copies[1:]:
        copy.wait()
    code_row = owner_codes(owner, count)
    table[...] = code_row
    parent = parents[:, pl.ds(pl.multiple_of(me * tok, tok), tok)]
    code, key = code_and_key(parent, code_row, me // CORES, chips)
    key_row = to_row(key)
    place = jnp.sum(jnp.where(key < key_row, 1.0, 0.0), axis=0, keepdims=True).astype(I32)
    pick = jnp.where(iota((tok, tok), 0) == place, 1.0, 0.0).astype(BF16)
    copies[0].wait()
    unit = unit_rms(points[...]).astype(BF16)
    ordered = jnp.dot(pick, unit, preferred_element_type=F32).astype(BF16)
    for (lo, hi), out_ref in zip(ranges, out_refs):
        out_ref[...] = ordered[lo:hi]


def codes_kernel(chips, starts, tok, wide, parents, table, out_ref):
    me = lax.axis_index("own")
    code_row = table[...]
    total = out_ref.shape[1]
    out = jnp.zeros((1, total), F32)
    for rel in range(total // wide):
        parent = parents[:, pl.ds(pl.multiple_of((me ^ rel) * tok, tok), tok)]
        code, key = code_and_key(parent, code_row, (me ^ rel) // CORES, chips)
        place = jnp.sum(jnp.where(to_row(key) < key, 1.0, 0.0), axis=1, keepdims=True).astype(I32)
        inside = iota((tok, total), 1) - rel * wide
        hit = (inside >= 0) & (inside < wide) & (place == inside + starts[chips - 1 - rel // CORES])
        out = out + jnp.sum(jnp.where(hit, code, 0.0), axis=0, keepdims=True)
    out_ref[...] = out


def cent_kernel(in_ref, out_ref, base_ref):
    out_ref[...] = unit_rms(in_ref[...]).astype(BF16)
    share = base_ref.shape[0]
    base_ref[...] = out_ref[pl.ds(pl.multiple_of(lax.axis_index("pts") * share, share), share), :]


def weights_kernel(places, tile, *refs):
    row_refs, (codes_ref, cent_ref, w_ref, sum_ref, rows_ref, low_ref, high_ref) = refs[:-7], refs[-7:]
    me = lax.axis_index("own")
    slots, width = cent_ref.shape
    total = codes_ref.shape[1]
    at = 0
    for row_ref, place in zip(row_refs, places):
        size = row_ref.shape[0]
        part = slice(at, at + size)
        at += size
        rows_ref[part, :] = row_ref[...]
        hit = iota((size, total), 1) == iota((size, total), 0) + place
        code = jnp.sum(jnp.where(hit, codes_ref[...], 0.0), axis=1, keepdims=True).astype(I32)
        first = (code % OWNER_SHIFT) // FIRST_SHIFT
        low = jnp.where(code // OWNER_SHIFT == me, first, slots)
        low_ref[part, :] = low
        high_ref[part, :] = low + code % FIRST_SHIFT

    def step(i, carry):
        at = pl.multiple_of(i * tile, tile)
        cent = cent_ref[pl.ds(at, tile), :]
        scores = lax.dot_general(rows_ref[...], cent, (((1,), (1,)), ((), ())), preferred_element_type=F32)
        slot = iota(scores.shape, 1) + at
        live = (slot >= low_ref[...]) & (slot < high_ref[...])
        w = jnp.where(live, jnp.exp(scores * (1.0 / (width * 0.05))), 0.0)
        w_ref[:, pl.ds(at, tile)] = w
        sum_ref[:, pl.ds(at, tile)] = jnp.sum(w, axis=0, keepdims=True)
        return carry

    lax.fori_loop(0, slots // tile, step, 0)


def inverse(values):
    return jnp.where(values > 0.0, 1.0 / jnp.where(values > 0.0, values, 1.0), 0.0)


def balance_kernel(n, *refs):
    w_refs, col_ref, out_ref = refs[:n], refs[n], refs[n + 1]
    scale = inverse(col_ref[...])
    total = jnp.zeros_like(scale)
    for w_ref in w_refs:
        rows = w_ref.shape[0]
        for at in range(0, rows, ROWS * 2):
            w = w_ref[at : at + ROWS * 2, :]
            row = jnp.sum(w * scale, axis=1, keepdims=True)
            total = total + jnp.sum(w * inverse(row), axis=0, keepdims=True)
    out_ref[...] = total


def assign_kernel(half_bit, *refs):
    w_refs, (t_ref, assign_ref) = refs[:-2], refs[-2:]
    scale = inverse(t_ref[...])
    half = assign_ref.shape[1]
    upper = (lax.axis_index("pts") // half_bit) % 2
    at = 0
    for w_ref in w_refs:
        for lo in range(0, w_ref.shape[0], ROWS * 2):
            w = w_ref[lo : lo + ROWS * 2, :] * scale
            row = inverse(jnp.sum(w, axis=1, keepdims=True))
            mine = jnp.where(upper == 0, w[:, :half], w[:, half:])
            assign_ref[at : at + ROWS * 2, :] = (mine * row).astype(BF16)
            at += ROWS * 2


def move_kernel(routes, half_bit, assign_ref, row_refs, out_refs, part_ref):
    low = lax.axis_index("pts") % half_bit
    for which, (order, out_ref) in enumerate(zip(routes, out_refs)):
        share, cols = out_ref.shape[1:]
        block = part_ref.shape[0]
        lanes = slice(which * cols, (which + 1) * cols)
        for k, rel in enumerate(order):
            start = (low ^ rel) * share
            columns = pl.ds(pl.multiple_of(start // block * block, block), block)
            moved, at = 0.0, 0
            for r in row_refs:
                a = assign_ref[at : at + r.shape[0], columns]
                moved = moved + lax.dot_general(
                    a, r[:, lanes], (((0,), (0,)), ((), ())), preferred_element_type=F32
                )
                at += r.shape[0]
            if share < block:
                part_ref[...] = moved
                moved = part_ref[pl.ds(pl.multiple_of(start % block, share), share), :]
            out_ref[k] = moved.astype(out_ref.dtype)


def send_kernel(routes, half_bit, nw, *refs):
    n = len(routes)
    row_refs, out_refs = refs[nw + 1 : -n - 2], refs[-n - 2 : -2]
    assign_ref, part_ref = refs[-2:]
    assign_kernel(half_bit, *refs[: nw + 1], assign_ref)
    move_kernel(routes, half_bit, assign_ref, row_refs, out_refs, part_ref)


def keep_kernel(routes, half_bit, *refs):
    n = len(routes)
    move_kernel(routes, half_bit, refs[0], refs[1 : -n - 1], refs[-n - 1 : -1], refs[-1])


def merge_kernel(keep_ref, came_ref, *out_refs):
    total = keep_ref[...] + came_ref[...].astype(F32)
    n = total.shape[0] // 2
    out_refs[0][...] = total[:n]
    out_refs[1][...] = total[n:].astype(BF16)


def final_kernel(nroute, nterm, *refs):
    base_ref, out_ref = refs[nroute * nterm], refs[nroute * nterm + 1]
    parts = []
    for which in range(nroute):
        total = refs[which * nterm][...].astype(F32)
        for k in range(1, nterm):
            total = total + refs[which * nterm + k][...].astype(F32)
        parts.append(total)
    moved = jnp.concatenate(parts, axis=1)
    out_ref[...] = unit_rms(base_ref[...].astype(F32) + 8.0 * moved).astype(BF16)


def call(kernel, outs, *args, scratch=(), vmem=16, where=pltpu.VMEM):
    shapes = [jax.ShapeDtypeStruct(s, d) for s, d in outs]
    size = sum(a.size * a.dtype.itemsize for a in args) + sum(s.size * s.dtype.itemsize for s in shapes)
    got = pl.pallas_call(
        kernel,
        out_shape=shapes,
        in_specs=[pl.BlockSpec(memory_space=where)] * len(args),
        out_specs=[pl.BlockSpec(memory_space=pltpu.VMEM)] * len(shapes),
        scratch_shapes=list(scratch),
        compiler_params=pltpu.CompilerParams(vmem_limit_bytes=vmem << 20),
        cost_estimate=pl.CostEstimate(flops=0, bytes_accessed=0, transcendentals=0),
    )(*args)
    return got[0] if len(shapes) == 1 else got


def after(values, gate):
    return lax.optimization_barrier((values, gate))[0]


def swap(values, axis, bit):
    return lax.ppermute(values, axis, [(i, i ^ bit) for i in range(lax.axis_size(axis))])


def powers(end):
    return [1 << k for k in range(end.bit_length() - 1)]


def bit_orders(bits):
    orders = []
    for k in range(len(bits)):
        order = bits[k:] + bits[:k]
        blocks = [0]
        for bit in reversed(order):
            blocks = blocks + [b | bit for b in blocks]
        orders.append((order, blocks))
    return orders


def local(points, parent_of, owner_of, child_count, centroids):
    owners, groups = lax.axis_size("own"), lax.axis_size("pts")
    chips = owners // CORES
    tok, width = points.shape
    slots = centroids.shape[1]
    share = slots // groups
    starts, wide, pieces, parts = windows(tok, owners)
    parents = parent_of.T
    table = [owner_of.reshape(1, -1), child_count.reshape(1, -1)]
    half_bit = groups // 2

    ranges = pieces + [(s, s + wide) for s in starts]
    *ordered, parents, codes = call(
        functools.partial(sort_kernel, chips, ranges),
        [((hi - lo, width), BF16) for lo, hi in ranges] + [(parents.shape, I32), (table[0].shape, F32)],
        points, parents, *table,
        scratch=[
            pltpu.VMEM((tok, width), BF16), *[pltpu.VMEM(a.shape, I32) for a in table],
            pltpu.SemaphoreType.DMA((4,)),
        ],
        where=pl.ANY, vmem=62,
    )
    held, whole = ordered[: len(pieces)], ordered[len(pieces) :]

    def place(chip, core, lo):
        return (chip * CORES + core) * wide + lo - starts[chips - 1 - chip]

    def weigh(rows, places, codes):
        count = sum(r.shape[0] for r in rows)
        return call(
            functools.partial(weights_kernel, places, min(slots, 256)),
            [((count, slots), F32), ((1, slots), F32), ((count, width), BF16)], *rows, codes, cent,
            scratch=[pltpu.VMEM((count, 1), I32), pltpu.VMEM((count, 1), I32)],
        )

    near = [whole[-1]] + [swap(whole[chips - 1 - chip], "own", chip * CORES) for chip in range(1, chips)]
    far_held = [swap(held[0], "pts", half_bit)]
    near = [(r, swap(r, "own", 1)) for r in near]
    codes = call(
        functools.partial(codes_kernel, chips, starts, tok, wide), [((1, owners * wide), F32)], parents, codes,
        vmem=4,
    )
    cent, base = call(cent_kernel, [((slots, width), BF16), ((share, width), BF16)], centroids[0])

    near_w, near_s, near_x = zip(*[
        weigh(
            near[chip], [place(chip, c, starts[chips - 1 - chip]) for c in range(CORES)],
            after(codes, far_held[0]) if chip else codes,
        )
        for chip in range(chips)
    ])

    def forward(k, gate):
        for chip in range(1, chips):
            if k in parts[chips - 1 - chip]:
                far_cross[chip, k] = swap(after(far_held[k], gate), "own", chip * CORES)

    def pair(chip, k, gate):
        rows = after(far_cross[chip, k] if chip else far_held[k], gate)
        for core, r in enumerate((rows, swap(rows, "own", 1))):
            far[int(k == parts[chips - 1 - chip][-1])].append((r, place(chip, core, pieces[k][0])))

    far, far_cross = [[], []], {}
    partial = sum(near_s)
    came = swap(jnp.concatenate([partial, codes], axis=1), "pts", half_bit)
    column, far_codes = partial + came[:, :slots], came[:, slots:]
    forward(0, partial)
    sums = [column]
    for bit in powers(half_bit):
        column = column + swap(column, "pts", bit)
        sums.append(column)
    far_held.append(swap(after(held[1], sums[0]), "pts", half_bit))
    for piece in held[2:]:
        far_held.append(swap(after(piece, sums[1]), "pts", half_bit))
    balance = call(functools.partial(balance_kernel, chips), [((1, slots), F32)], *near_w, column)
    balance = after(balance, [far_cross[chip, 0] for chip in range(1, chips) if (chip, 0) in far_cross])
    steps = [balance]
    for bit in powers(groups):
        balance = balance + swap(balance, "pts", bit)
        steps.append(balance)
    for k in range(1, len(pieces)):
        forward(k, steps[1])
    for chip in range(chips):
        mine = parts[chips - 1 - chip]
        for k in mine:
            pair(chip, k, steps[-2] if k == mine[-1] else steps[0])
    far_w, _, far_x = zip(*[
        weigh([r for r, _ in rows], [p for _, p in rows], after(far_codes, gate))
        for rows, gate in zip(far, (steps[1], steps[-2]))
    ])

    bits = powers(half_bit)
    orders = bit_orders(bits)
    cols = width // len(orders)
    m = half_bit // 2
    rows = [*near_x, *far_x]
    total_rows = sum(r.shape[0] for r in rows)
    part = pltpu.VMEM((max(share, LANES), cols), F32)
    got = call(
        functools.partial(send_kernel, [b[m:] for _, b in orders], half_bit, len(near_w) + len(far_w)),
        [((m, share, cols), BF16)] * len(orders) + [((total_rows, slots // 2), BF16)],
        *near_w, *far_w, balance, *rows, scratch=[part],
    )
    sends, assign = got[:-1], got[-1]
    keeps = call(
        functools.partial(keep_kernel, [b[:m] for _, b in orders], half_bit),
        [((m, share, cols), F32)] * len(orders), assign, *rows, scratch=[part],
    )
    keeps = list(keeps) if len(orders) > 1 else [keeps]
    last = []
    for step in range(len(bits)):
        came = [swap(s, "pts", orders[r][0][step]) for r, s in enumerate(sends)]
        n = came[0].shape[0] // 2
        if n == 0:
            last = came
            break
        sends = []
        for r, c in enumerate(came):
            keeps[r], send = call(
                merge_kernel, [((n, share, cols), F32), ((n, share, cols), BF16)], keeps[r], c, vmem=8
            )
            sends.append(send)
    flat = [t.reshape(share, cols) for pair in zip(keeps, last) for t in pair]
    out = call(
        functools.partial(final_kernel, len(orders), 2), [((share, width), BF16)], *flat, base, vmem=8
    )
    return out[None]


def solution(mesh):
    in_specs = (P(("pts", "own"), None), P("pts", None), P(), P(), P("own", None, None))
    out_specs = P("own", "pts", None)
    return jax.shard_map(local, mesh=mesh, in_specs=in_specs, out_specs=out_specs, check_vma=False)
```

```python
import functools

import jax
import jax.numpy as jnp
from jax import lax
from jax.experimental import pallas as pl
from jax.experimental.pallas import tpu as pltpu
from jax.sharding import PartitionSpec as P

F32 = jnp.float32
BF16 = jnp.bfloat16
I32 = jnp.int32
CORES = 2
ROWS = 16
LANES = 128
OWNER_SHIFT = 1 << 17
FIRST_SHIFT = 1 << 7


def down(value):
    return value // ROWS * ROWS


def up(value):
    return -(-value // ROWS) * ROWS


def iota(shape, dim):
    return lax.broadcasted_iota(I32, shape, dim)


def unit_rms(values):
    values = values.astype(F32)
    return values * lax.rsqrt(jnp.mean(values * values, axis=-1, keepdims=True) + 1e-06)


def windows(tok, owners):
    chips = owners // CORES
    full = 2 * tok // owners
    least = CORES * ((tok - full) // max(owners - 1, 1))
    starts = [down(j * least) for j in range(chips)]
    ends = [up(tok - (chips - 1 - j) * least) for j in range(chips)]
    wide = max(e - s for s, e in zip(starts, ends))
    starts = [min(s, tok - wide) for s in starts]
    starts = [min(s, tok - wide) for s in starts]
    cuts = sorted(set(starts + [s + wide for s in starts] + [0, tok]))
    pieces = list(zip(cuts[:-1], cuts[1:]))
    parts = [[k for k, (lo, hi) in enumerate(pieces) if s <= lo and hi <= s + wide] for s in starts]
    return starts, wide, pieces, parts


def to_col(row):
    n = row.shape[1]
    return jnp.sum(jnp.where(iota((n, n), 0) == iota((n, n), 1), row, 0.0), axis=1, keepdims=True)


def to_row(col):
    n = col.shape[0]
    return jnp.sum(jnp.where(iota((n, n), 0) == iota((n, n), 1), col, 0.0), axis=0, keepdims=True)


def owner_codes(owner_ref, count_ref):
    owner = owner_ref[...].astype(F32)
    count = count_ref[...].astype(F32)
    n = owner.shape[1]
    earlier = (to_col(owner) == owner) & (iota((n, n), 0) < iota((n, n), 1))
    first = jnp.sum(jnp.where(earlier, to_col(count), 0.0), axis=0, keepdims=True)
    return owner * OWNER_SHIFT + first * FIRST_SHIFT + count


def code_and_key(parent_row, code_row, chip, chips):
    parent = to_col(parent_row.astype(F32)).astype(I32)
    tok = parent.shape[0]
    n = code_row.shape[1]
    code = jnp.sum(jnp.where(parent == iota((tok, n), 1), code_row, 0.0), axis=1, keepdims=True)
    owner = code.astype(I32) // OWNER_SHIFT
    order = (chips - 1) - ((owner // CORES) ^ chip)
    key = (order * tok + iota((tok, 1), 0)).astype(F32)
    return code, key


def fetch(pairs, sems):
    copies = [pltpu.make_async_copy(src, dst, sems.at[k]) for k, (src, dst) in enumerate(pairs)]
    for copy in copies:
        copy.start()
    return copies


def sort_kernel(chips, ranges, *refs):
    points_ref, parents_ref, owner_ref, count_ref = refs[:4]
    out_refs, (parents, table, points, owner, count, sems) = refs[4:-6], refs[-6:]
    copies = fetch(
        [(points_ref, points), (parents_ref, parents), (owner_ref, owner), (count_ref, count)], sems
    )
    me = lax.axis_index("own")
    tok = points.shape[0]
    for copy in copies[1:]:
        copy.wait()
    code_row = owner_codes(owner, count)
    table[...] = code_row
    parent = parents[:, pl.ds(pl.multiple_of(me * tok, tok), tok)]
    code, key = code_and_key(parent, code_row, me // CORES, chips)
    key_row = to_row(key)
    place = jnp.sum(jnp.where(key < key_row, 1.0, 0.0), axis=0, keepdims=True).astype(I32)
    pick = jnp.where(iota((tok, tok), 0) == place, 1.0, 0.0).astype(BF16)
    copies[0].wait()
    unit = unit_rms(points[...]).astype(BF16)
    ordered = jnp.dot(pick, unit, preferred_element_type=F32).astype(BF16)
    for (lo, hi), out_ref in zip(ranges, out_refs):
        out_ref[...] = ordered[lo:hi]


def codes_kernel(chips, starts, tok, wide, parents, table, out_ref):
    me = lax.axis_index("own")
    code_row = table[...]
    total = out_ref.shape[1]
    out = jnp.zeros((1, total), F32)
    for rel in range(total // wide):
        parent = parents[:, pl.ds(pl.multiple_of((me ^ rel) * tok, tok), tok)]
        code, key = code_and_key(parent, code_row, (me ^ rel) // CORES, chips)
        place = jnp.sum(jnp.where(to_row(key) < key, 1.0, 0.0), axis=1, keepdims=True).astype(I32)
        inside = iota((tok, total), 1) - rel * wide
        hit = (inside >= 0) & (inside < wide) & (place == inside + starts[chips - 1 - rel // CORES])
        out = out + jnp.sum(jnp.where(hit, code, 0.0), axis=0, keepdims=True)
    out_ref[...] = out


def cent_kernel(in_ref, out_ref, base_ref):
    out_ref[...] = unit_rms(in_ref[...]).astype(BF16)
    share = base_ref.shape[0]
    base_ref[...] = out_ref[pl.ds(pl.multiple_of(lax.axis_index("pts") * share, share), share), :]


def weights_kernel(places, tile, *refs):
    row_refs, (codes_ref, cent_ref, w_ref, sum_ref, rows_ref, low_ref, high_ref) = refs[:-7], refs[-7:]
    me = lax.axis_index("own")
    slots, width = cent_ref.shape
    total = codes_ref.shape[1]
    at = 0
    for row_ref, place in zip(row_refs, places):
        size = row_ref.shape[0]
        part = slice(at, at + size)
        at += size
        rows_ref[part, :] = row_ref[...]
        hit = iota((size, total), 1) == iota((size, total), 0) + place
        code = jnp.sum(jnp.where(hit, codes_ref[...], 0.0), axis=1, keepdims=True).astype(I32)
        first = (code % OWNER_SHIFT) // FIRST_SHIFT
        low = jnp.where(code // OWNER_SHIFT == me, first, slots)
        low_ref[part, :] = low
        high_ref[part, :] = low + code % FIRST_SHIFT

    def step(i, carry):
        at = pl.multiple_of(i * tile, tile)
        cent = cent_ref[pl.ds(at, tile), :]
        scores = lax.dot_general(rows_ref[...], cent, (((1,), (1,)), ((), ())), preferred_element_type=F32)
        slot = iota(scores.shape, 1) + at
        live = (slot >= low_ref[...]) & (slot < high_ref[...])
        w = jnp.where(live, jnp.exp(scores * (1.0 / (width * 0.05))), 0.0)
        w_ref[:, pl.ds(at, tile)] = w
        sum_ref[:, pl.ds(at, tile)] = jnp.sum(w, axis=0, keepdims=True)
        return carry

    lax.fori_loop(0, slots // tile, step, 0)


def inverse(values):
    return jnp.where(values > 0.0, 1.0 / jnp.where(values > 0.0, values, 1.0), 0.0)


def balance_kernel(n, *refs):
    w_refs, col_ref, out_ref = refs[:n], refs[n], refs[n + 1]
    scale = inverse(col_ref[...])
    total = jnp.zeros_like(scale)
    for w_ref in w_refs:
        rows = w_ref.shape[0]
        for at in range(0, rows, ROWS * 2):
            w = w_ref[at : at + ROWS * 2, :]
            row = jnp.sum(w * scale, axis=1, keepdims=True)
            total = total + jnp.sum(w * inverse(row), axis=0, keepdims=True)
    out_ref[...] = total


def assign_kernel(half_bit, *refs):
    w_refs, (t_ref, assign_ref) = refs[:-2], refs[-2:]
    scale = inverse(t_ref[...])
    half = assign_ref.shape[1]
    upper = (lax.axis_index("pts") // half_bit) % 2
    at = 0
    for w_ref in w_refs:
        for lo in range(0, w_ref.shape[0], ROWS * 2):
            w = w_ref[lo : lo + ROWS * 2, :] * scale
            row = inverse(jnp.sum(w, axis=1, keepdims=True))
            mine = jnp.where(upper == 0, w[:, :half], w[:, half:])
            assign_ref[at : at + ROWS * 2, :] = (mine * row).astype(BF16)
            at += ROWS * 2


def move_kernel(routes, half_bit, assign_ref, row_refs, out_refs, part_ref):
    low = lax.axis_index("pts") % half_bit
    for which, (order, out_ref) in enumerate(zip(routes, out_refs)):
        share, cols = out_ref.shape[1:]
        block = part_ref.shape[0]
        lanes = slice(which * cols, (which + 1) * cols)
        for k, rel in enumerate(order):
            start = (low ^ rel) * share
            columns = pl.ds(pl.multiple_of(start // block * block, block), block)
            moved, at = 0.0, 0
            for r in row_refs:
                a = assign_ref[at : at + r.shape[0], columns]
                moved = moved + lax.dot_general(
                    a, r[:, lanes], (((0,), (0,)), ((), ())), preferred_element_type=F32
                )
                at += r.shape[0]
            if share < block:
                part_ref[...] = moved
                moved = part_ref[pl.ds(pl.multiple_of(start % block, share), share), :]
            out_ref[k] = moved.astype(out_ref.dtype)


def send_kernel(routes, half_bit, nw, *refs):
    n = len(routes)
    row_refs, out_refs = refs[nw + 1 : -n - 2], refs[-n - 2 : -2]
    assign_ref, part_ref = refs[-2:]
    assign_kernel(half_bit, *refs[: nw + 1], assign_ref)
    move_kernel(routes, half_bit, assign_ref, row_refs, out_refs, part_ref)


def keep_kernel(routes, half_bit, *refs):
    n = len(routes)
    move_kernel(routes, half_bit, refs[0], refs[1 : -n - 1], refs[-n - 1 : -1], refs[-1])


def merge_kernel(keep_ref, came_ref, *out_refs):
    total = keep_ref[...] + came_ref[...].astype(F32)
    n = total.shape[0] // 2
    out_refs[0][...] = total[:n]
    out_refs[1][...] = total[n:].astype(BF16)


def final_kernel(nroute, nterm, *refs):
    base_ref, out_ref = refs[nroute * nterm], refs[nroute * nterm + 1]
    parts = []
    for which in range(nroute):
        total = refs[which * nterm][...].astype(F32)
        for k in range(1, nterm):
            total = total + refs[which * nterm + k][...].astype(F32)
        parts.append(total)
    moved = jnp.concatenate(parts, axis=1)
    out_ref[...] = unit_rms(base_ref[...].astype(F32) + 8.0 * moved).astype(BF16)


def call(kernel, outs, *args, scratch=(), vmem=16, where=pltpu.VMEM):
    shapes = [jax.ShapeDtypeStruct(s, d) for s, d in outs]
    size = sum(a.size * a.dtype.itemsize for a in args) + sum(s.size * s.dtype.itemsize for s in shapes)
    got = pl.pallas_call(
        kernel,
        out_shape=shapes,
        in_specs=[pl.BlockSpec(memory_space=where)] * len(args),
        out_specs=[pl.BlockSpec(memory_space=pltpu.VMEM)] * len(shapes),
        scratch_shapes=list(scratch),
        compiler_params=pltpu.CompilerParams(vmem_limit_bytes=vmem << 20),
        cost_estimate=pl.CostEstimate(flops=0, bytes_accessed=0, transcendentals=0),
    )(*args)
    return got[0] if len(shapes) == 1 else got


def after(values, gate):
    return lax.optimization_barrier((values, gate))[0]


def swap(values, axis, bit):
    return lax.ppermute(values, axis, [(i, i ^ bit) for i in range(lax.axis_size(axis))])


def powers(end):
    return [1 << k for k in range(end.bit_length() - 1)]


def bit_orders(bits):
    orders = []
    for k in range(len(bits)):
        order = bits[k:] + bits[:k]
        blocks = [0]
        for bit in reversed(order):
            blocks = blocks + [b | bit for b in blocks]
        orders.append((order, blocks))
    return orders


def local(points, parent_of, owner_of, child_count, centroids):
    owners, groups = lax.axis_size("own"), lax.axis_size("pts")
    chips = owners // CORES
    tok, width = points.shape
    slots = centroids.shape[1]
    share = slots // groups
    starts, wide, pieces, parts = windows(tok, owners)
    parents = parent_of.T
    table = [owner_of.reshape(1, -1), child_count.reshape(1, -1)]
    half_bit = groups // 2

    ranges = pieces + [(s, s + wide) for s in starts]
    *ordered, parents, codes = call(
        functools.partial(sort_kernel, chips, ranges),
        [((hi - lo, width), BF16) for lo, hi in ranges] + [(parents.shape, I32), (table[0].shape, F32)],
        points, parents, *table,
        scratch=[
            pltpu.VMEM((tok, width), BF16), *[pltpu.VMEM(a.shape, I32) for a in table],
            pltpu.SemaphoreType.DMA((4,)),
        ],
        where=pl.ANY, vmem=62,
    )
    held, whole = ordered[: len(pieces)], ordered[len(pieces) :]

    def place(chip, core, lo):
        return (chip * CORES + core) * wide + lo - starts[chips - 1 - chip]

    def weigh(rows, places, codes):
        count = sum(r.shape[0] for r in rows)
        return call(
            functools.partial(weights_kernel, places, min(slots, 256)),
            [((count, slots), F32), ((1, slots), F32), ((count, width), BF16)], *rows, codes, cent,
            scratch=[pltpu.VMEM((count, 1), I32), pltpu.VMEM((count, 1), I32)],
        )

    near = [whole[-1]] + [swap(whole[chips - 1 - chip], "own", chip * CORES) for chip in range(1, chips)]
    far_held = [swap(held[0], "pts", half_bit)]
    codes = call(
        functools.partial(codes_kernel, chips, starts, tok, wide), [((1, owners * wide), F32)], parents, codes,
        vmem=4,
    )
    cent, base = call(cent_kernel, [((slots, width), BF16), ((share, width), BF16)], centroids[0])

    far_codes = swap(codes, "pts", half_bit)

    def weigh_near(chip, rows, codes):
        start = starts[chips - 1 - chip]
        return weigh((rows, swap(rows, "own", 1)), [place(chip, c, start) for c in range(CORES)], codes)

    near_got = [weigh_near(0, near[0], codes)]
    first = near_got[0][1]
    for chip in range(1, chips):
        near_got.append(weigh_near(chip, after(near[chip], (first, far_held[0], far_codes)), codes))
    near_w, near_s, near_x = zip(*near_got)

    def forward(k, gate):
        for chip in range(1, chips):
            if k in parts[chips - 1 - chip]:
                far_cross[chip, k] = swap(after(far_held[k], gate), "own", chip * CORES)

    def pair(chip, k, gate):
        rows = after(far_cross[chip, k] if chip else far_held[k], gate)
        for core, r in enumerate((rows, swap(rows, "own", 1))):
            far[int(k == parts[chips - 1 - chip][-1])].append((r, place(chip, core, pieces[k][0])))

    def weigh_far(late, gate):
        rows = far[late]
        return weigh([r for r, _ in rows], [p for _, p in rows], after(far_codes, gate))

    far, far_cross = [[], []], {}
    partial = sum(near_s)
    masks = powers(half_bit) + [half_bit | half_bit >> 1]
    far_held.append(swap(after(held[1], first), "pts", half_bit))
    forward(0, partial)
    sums = [partial]
    here = [far_cross[c, 0] for c in range(1, chips) if (c, 0) in far_cross]
    for mask in masks[:-1]:
        sums.append(sums[-1] + swap(sums[-1], "pts", mask))
    sums.append(sums[-1] + swap(after(sums[-1], here), "pts", masks[-1]))
    column = sums[-1]
    for piece in held[2:]:
        far_held.append(swap(after(piece, first), "pts", half_bit))
    balance = call(functools.partial(balance_kernel, chips), [((1, slots), F32)], *near_w, column)
    steps = [balance]
    for k, mask in enumerate(masks[:-1]):
        balance = balance + swap(balance, "pts", mask)
        steps.append(balance)
    for k in range(1, len(pieces)):
        forward(k, column)
    for chip in range(chips):
        mine = parts[chips - 1 - chip]
        for k in mine:
            pair(chip, k, steps[-1] if k == mine[-1] else steps[0])
    far_got = [weigh_far(0, steps[1])]
    balance = balance + swap(after(balance, far_got[0][0]), "pts", masks[-1])
    far_got.append(weigh_far(1, steps[-1]))
    far_w, far_x = zip(*[(w, x) for w, _, x in far_got])

    bits = powers(half_bit)
    orders = bit_orders(bits)
    cols = width // len(orders)
    m = half_bit // 2
    rows = [*near_x, *far_x]
    total_rows = sum(r.shape[0] for r in rows)
    part = pltpu.VMEM((max(share, LANES), cols), F32)
    got = call(
        functools.partial(send_kernel, [b[m:] for _, b in orders], half_bit, len(near_w) + len(far_w)),
        [((m, share, cols), BF16)] * len(orders) + [((total_rows, slots // 2), BF16)],
        *near_w, *far_w, balance, *rows, scratch=[part],
    )
    sends, assign = got[:-1], got[-1]
    keeps = call(
        functools.partial(keep_kernel, [b[:m] for _, b in orders], half_bit),
        [((m, share, cols), F32)] * len(orders), assign, *rows, scratch=[part],
    )
    keeps = list(keeps) if len(orders) > 1 else [keeps]
    last = []
    for step in range(len(bits)):
        came = [swap(s, "pts", orders[r][0][step]) for r, s in enumerate(sends)]
        n = came[0].shape[0] // 2
        if n == 0:
            last = came
            break
        sends = []
        for r, c in enumerate(came):
            keeps[r], send = call(
                merge_kernel, [((n, share, cols), F32), ((n, share, cols), BF16)], keeps[r], c, vmem=8
            )
            sends.append(send)
    flat = [t.reshape(share, cols) for pair in zip(keeps, last) for t in pair]
    out = call(
        functools.partial(final_kernel, len(orders), 2), [((share, width), BF16)], *flat, base, vmem=8
    )
    return out[None]


def solution(mesh):
    in_specs = (P(("pts", "own"), None), P("pts", None), P(), P(), P("own", None, None))
    out_specs = P("own", "pts", None)
    return jax.shard_map(local, mesh=mesh, in_specs=in_specs, out_specs=out_specs, check_vma=False)
```

```python
import functools

import jax
import jax.numpy as jnp
from jax import lax
from jax.experimental import pallas as pl
from jax.experimental.pallas import tpu as pltpu
from jax.sharding import PartitionSpec as P

F32 = jnp.float32
BF16 = jnp.bfloat16
I32 = jnp.int32
CORES = 2
ROWS = 16
LANES = 128
OWNER_SHIFT = 1 << 17
FIRST_SHIFT = 1 << 7


def down(value):
    return value // ROWS * ROWS


def up(value):
    return -(-value // ROWS) * ROWS


def iota(shape, dim):
    return lax.broadcasted_iota(I32, shape, dim)


def unit_rms(values):
    values = values.astype(F32)
    return values * lax.rsqrt(jnp.mean(values * values, axis=-1, keepdims=True) + 1e-06)


def windows(tok, owners):
    chips = owners // CORES
    full = 2 * tok // owners
    least = CORES * ((tok - full) // max(owners - 1, 1))
    starts = [down(j * least) for j in range(chips)]
    ends = [up(tok - (chips - 1 - j) * least) for j in range(chips)]
    wide = max(e - s for s, e in zip(starts, ends))
    starts = [min(s, tok - wide) for s in starts]
    starts = [min(s, tok - wide) for s in starts]
    soon = down(starts[min(1, chips - 1)] * 13 // 16)
    cuts = sorted({0, soon, tok} | {s + wide for s in starts})
    pieces = list(zip(cuts[:-1], cuts[1:]))
    parts = [[k for k, (lo, hi) in enumerate(pieces) if lo < s + wide and s < hi] for s in starts]
    return starts, wide, pieces, parts


def to_col(row):
    n = row.shape[1]
    return jnp.sum(jnp.where(iota((n, n), 0) == iota((n, n), 1), row, 0.0), axis=1, keepdims=True)


def to_row(col):
    n = col.shape[0]
    return jnp.sum(jnp.where(iota((n, n), 0) == iota((n, n), 1), col, 0.0), axis=0, keepdims=True)


def owner_codes(owner_ref, count_ref):
    owner = owner_ref[...].astype(F32)
    count = count_ref[...].astype(F32)
    n = owner.shape[1]
    earlier = (to_col(owner) == owner) & (iota((n, n), 0) < iota((n, n), 1))
    first = jnp.sum(jnp.where(earlier, to_col(count), 0.0), axis=0, keepdims=True)
    return owner * OWNER_SHIFT + first * FIRST_SHIFT + count


def code_and_key(parent_row, code_row, chip, chips):
    parent = to_col(parent_row.astype(F32)).astype(I32)
    tok = parent.shape[0]
    n = code_row.shape[1]
    code = jnp.sum(jnp.where(parent == iota((tok, n), 1), code_row, 0.0), axis=1, keepdims=True)
    owner = code.astype(I32) // OWNER_SHIFT
    order = (chips - 1) - ((owner // CORES) ^ chip)
    key = (order * tok + iota((tok, 1), 0)).astype(F32)
    return code, key


def fetch(pairs, sems):
    copies = [pltpu.make_async_copy(src, dst, sems.at[k]) for k, (src, dst) in enumerate(pairs)]
    for copy in copies:
        copy.start()
    return copies


def sort_kernel(chips, ranges, *refs):
    points_ref, parents_ref, owner_ref, count_ref = refs[:4]
    out_refs, (parents, table, points, owner, count, sems) = refs[4:-6], refs[-6:]
    copies = fetch(
        [(points_ref, points), (parents_ref, parents), (owner_ref, owner), (count_ref, count)], sems
    )
    me = lax.axis_index("own")
    tok = points.shape[0]
    for copy in copies[1:]:
        copy.wait()
    code_row = owner_codes(owner, count)
    table[...] = code_row
    parent = parents[:, pl.ds(pl.multiple_of(me * tok, tok), tok)]
    code, key = code_and_key(parent, code_row, me // CORES, chips)
    key_row = to_row(key)
    place = jnp.sum(jnp.where(key < key_row, 1.0, 0.0), axis=0, keepdims=True).astype(I32)
    pick = jnp.where(iota((tok, tok), 0) == place, 1.0, 0.0).astype(BF16)
    copies[0].wait()
    unit = unit_rms(points[...]).astype(BF16)
    ordered = jnp.dot(pick, unit, preferred_element_type=F32).astype(BF16)
    for (lo, hi), out_ref in zip(ranges, out_refs):
        out_ref[...] = ordered[lo:hi]


def codes_kernel(chips, starts, tok, wide, parents, table, out_ref):
    me = lax.axis_index("own")
    code_row = table[...]
    total = out_ref.shape[1]
    out = jnp.zeros((1, total), F32)
    for rel in range(total // wide):
        parent = parents[:, pl.ds(pl.multiple_of((me ^ rel) * tok, tok), tok)]
        code, key = code_and_key(parent, code_row, (me ^ rel) // CORES, chips)
        place = jnp.sum(jnp.where(to_row(key) < key, 1.0, 0.0), axis=1, keepdims=True).astype(I32)
        inside = iota((tok, total), 1) - rel * wide
        hit = (inside >= 0) & (inside < wide) & (place == inside + starts[chips - 1 - rel // CORES])
        out = out + jnp.sum(jnp.where(hit, code, 0.0), axis=0, keepdims=True)
    out_ref[...] = out


def cent_kernel(in_ref, out_ref, base_ref):
    out_ref[...] = unit_rms(in_ref[...]).astype(BF16)
    share = base_ref.shape[0]
    base_ref[...] = out_ref[pl.ds(pl.multiple_of(lax.axis_index("pts") * share, share), share), :]


def weights_kernel(places, tile, *refs):
    row_refs, (codes_ref, cent_ref, w_ref, sum_ref, rows_ref, low_ref, high_ref) = refs[:-7], refs[-7:]
    me = lax.axis_index("own")
    slots, width = cent_ref.shape
    total = codes_ref.shape[1]
    at = 0
    for row_ref, (place, skip, size) in zip(row_refs, places):
        part = slice(at, at + size)
        at += size
        rows_ref[part, :] = row_ref[skip : skip + size, :]
        hit = iota((size, total), 1) == iota((size, total), 0) + place
        code = jnp.sum(jnp.where(hit, codes_ref[...], 0.0), axis=1, keepdims=True).astype(I32)
        first = (code % OWNER_SHIFT) // FIRST_SHIFT
        low = jnp.where(code // OWNER_SHIFT == me, first, slots)
        low_ref[part, :] = low
        high_ref[part, :] = low + code % FIRST_SHIFT

    def step(i, carry):
        at = pl.multiple_of(i * tile, tile)
        cent = cent_ref[pl.ds(at, tile), :]
        scores = lax.dot_general(rows_ref[...], cent, (((1,), (1,)), ((), ())), preferred_element_type=F32)
        slot = iota(scores.shape, 1) + at
        live = (slot >= low_ref[...]) & (slot < high_ref[...])
        w = jnp.where(live, jnp.exp(scores * (1.0 / (width * 0.05))), 0.0)
        w_ref[:, pl.ds(at, tile)] = w
        sum_ref[:, pl.ds(at, tile)] = jnp.sum(w, axis=0, keepdims=True)
        return carry

    lax.fori_loop(0, slots // tile, step, 0, unroll=True)


def inverse(values):
    return jnp.where(values > 0.0, 1.0 / jnp.where(values > 0.0, values, 1.0), 0.0)


def balance_kernel(n, *refs):
    w_refs, col_ref, out_ref = refs[:n], refs[n], refs[n + 1]
    scale = inverse(col_ref[...])
    total = jnp.zeros_like(scale)
    for w_ref in w_refs:
        rows = w_ref.shape[0]
        for at in range(0, rows, ROWS * 2):
            w = w_ref[at : at + ROWS * 2, :]
            row = jnp.sum(w * scale, axis=1, keepdims=True)
            total = total + jnp.sum(w * inverse(row), axis=0, keepdims=True)
    out_ref[...] = total


def assign_kernel(half_bit, *refs):
    w_refs, (t_ref, assign_ref) = refs[:-2], refs[-2:]
    scale = inverse(t_ref[...])
    half = assign_ref.shape[1]
    upper = (lax.axis_index("pts") // half_bit) % 2
    at = 0
    for w_ref in w_refs:
        for lo in range(0, w_ref.shape[0], ROWS * 2):
            w = w_ref[lo : lo + ROWS * 2, :] * scale
            row = inverse(jnp.sum(w, axis=1, keepdims=True))
            mine = jnp.where(upper == 0, w[:, :half], w[:, half:])
            assign_ref[at : at + ROWS * 2, :] = (mine * row).astype(BF16)
            at += ROWS * 2


def move_kernel(wanted, half_bit, assign_ref, row_refs, out_refs, part_ref):
    low = lax.axis_index("pts") % half_bit
    for (which, order), out_ref in zip(wanted, out_refs):
        share, cols = out_ref.shape[1:]
        block = part_ref.shape[0]
        lanes = slice(which * cols, (which + 1) * cols)
        for k, rel in enumerate(order):
            start = (low ^ rel) * share
            columns = pl.ds(pl.multiple_of(start // block * block, block), block)
            moved, at = 0.0, 0
            for r in row_refs:
                a = assign_ref[at : at + r.shape[0], columns]
                moved = moved + lax.dot_general(
                    a, r[:, lanes], (((0,), (0,)), ((), ())), preferred_element_type=F32
                )
                at += r.shape[0]
            if share < block:
                part_ref[...] = moved
                moved = part_ref[pl.ds(pl.multiple_of(start % block, share), share), :]
            out_ref[k] = moved.astype(out_ref.dtype)


def send_kernel(wanted, half_bit, nw, *refs):
    n = len(wanted)
    row_refs, out_refs = refs[nw + 1 : -n - 2], refs[-n - 2 : -2]
    assign_ref, part_ref = refs[-2:]
    assign_kernel(half_bit, *refs[: nw + 1], assign_ref)
    move_kernel(wanted, half_bit, assign_ref, row_refs, out_refs, part_ref)


def keep_kernel(wanted, half_bit, *refs):
    n = len(wanted)
    move_kernel(wanted, half_bit, refs[0], refs[1 : -n - 1], refs[-n - 1 : -1], refs[-1])


def forward_kernel(keep_ref, came_ref, *out_refs):
    n = came_ref.shape[0]
    total = (keep_ref[n:] + came_ref[...].astype(F32)).astype(BF16)
    at = n
    for out_ref in out_refs:
        at -= out_ref.shape[0]
        out_ref[...] = total[at : at + out_ref.shape[0]]


def merge_kernel(keep_ref, came_ref, out_ref):
    out_ref[...] = keep_ref[: came_ref.shape[0]] + came_ref[...].astype(F32)


def final_kernel(nroute, nterm, *refs):
    base_ref, out_ref = refs[nroute * nterm], refs[nroute * nterm + 1]
    parts = []
    for which in range(nroute):
        total = 0.0
        for ref in refs[which * nterm : (which + 1) * nterm]:
            total = total + ref[0].astype(F32)
        parts.append(total)
    moved = jnp.concatenate(parts, axis=1)
    out_ref[...] = unit_rms(base_ref[...].astype(F32) + 8.0 * moved).astype(BF16)


def call(kernel, outs, *args, scratch=(), flops=0, vmem=16, where=pltpu.VMEM):
    shapes = [jax.ShapeDtypeStruct(s, d) for s, d in outs]
    size = sum(a.size * a.dtype.itemsize for a in args) + sum(s.size * s.dtype.itemsize for s in shapes)
    got = pl.pallas_call(
        kernel,
        out_shape=shapes,
        in_specs=[pl.BlockSpec(memory_space=where)] * len(args),
        out_specs=[pl.BlockSpec(memory_space=pltpu.VMEM)] * len(shapes),
        scratch_shapes=list(scratch),
        compiler_params=pltpu.CompilerParams(vmem_limit_bytes=vmem << 20),
        cost_estimate=pl.CostEstimate(flops=flops, bytes_accessed=0, transcendentals=0),
    )(*args)
    return got[0] if len(shapes) == 1 else got


def after(values, gate):
    return lax.optimization_barrier((values, gate))[0]


def swap(values, axis, bit):
    return lax.ppermute(values, axis, [(i, i ^ bit) for i in range(lax.axis_size(axis))])


def powers(end):
    return [1 << k for k in range(end.bit_length() - 1)]


def bit_orders(bits):
    orders = []
    for k in range(len(bits)):
        order = bits[k:] + bits[:k]
        blocks = [0]
        for bit in reversed(order):
            blocks = blocks + [b | bit for b in blocks]
        orders.append((order, blocks))
    return orders


def local(points, parent_of, owner_of, child_count, centroids):
    owners, groups = lax.axis_size("own"), lax.axis_size("pts")
    chips = owners // CORES
    tok, width = points.shape
    slots = centroids.shape[1]
    share = slots // groups
    starts, wide, pieces, parts = windows(tok, owners)
    parents = parent_of.T
    table = [owner_of.reshape(1, -1), child_count.reshape(1, -1)]
    half_bit = groups // 2
    far_mask = half_bit | half_bit >> 1

    ranges = pieces + [(s, s + wide) for s in starts]
    *ordered, parents, codes = call(
        functools.partial(sort_kernel, chips, ranges),
        [((hi - lo, width), BF16) for lo, hi in ranges] + [(parents.shape, I32), (table[0].shape, F32)],
        points, parents, *table,
        scratch=[
            pltpu.VMEM((tok, width), BF16), *[pltpu.VMEM(a.shape, I32) for a in table],
            pltpu.SemaphoreType.DMA((4,)),
        ],
        where=pl.ANY, vmem=62,
    )
    held, whole = ordered[: len(pieces)], ordered[len(pieces) :]

    def place(chip, core, lo, hi):
        start = starts[chips - 1 - chip]
        first, last = max(lo, start), min(hi, start + wide)
        return (chip * CORES + core) * wide + first - start, first - lo, last - first

    def weigh(rows, places, codes, flops=0):
        count = sum(size for _, _, size in places)
        return call(
            functools.partial(weights_kernel, places, min(slots, 256)),
            [((count, slots), F32), ((1, slots), F32), ((count, width), BF16)], *rows, codes, cent,
            scratch=[pltpu.VMEM((count, 1), I32), pltpu.VMEM((count, 1), I32)], flops=flops * count,
        )

    near = [whole[-1]] + [swap(whole[chips - 1 - chip], "own", chip * CORES) for chip in range(1, chips)]
    far_held = [swap(held[0], "pts", far_mask)]
    codes = call(
        functools.partial(codes_kernel, chips, starts, tok, wide), [((1, owners * wide), F32)], parents, codes,
        vmem=4,
    )
    cent, base = call(cent_kernel, [((slots, width), BF16), ((share, width), BF16)], centroids[0])

    far_codes = swap(codes, "pts", far_mask)

    def weigh_near(chip, rows, codes):
        start = starts[chips - 1 - chip]
        return weigh((rows, swap(rows, "own", 1)), [place(chip, c, start, start + wide) for c in range(CORES)], codes)

    near_got = [weigh_near(0, near[0], codes)]
    first = near_got[0][1]
    for chip in range(1, chips):
        near_got.append(weigh_near(chip, after(near[chip], (first, far_held[0], far_codes)), codes))
    near_w, near_s, near_x = zip(*near_got)

    def forward(k, gate):
        for chip in range(1, chips):
            if k in parts[chips - 1 - chip]:
                far_cross[chip, k] = swap(after(far_held[k], gate), "own", chip * CORES)

    def pair(chip, k, gate):
        rows = after(far_cross[chip, k] if chip else far_held[k], gate)
        for core, r in enumerate((rows, swap(rows, "own", 1))):
            far[int(k == parts[chips - 1 - chip][-1])].append((r, place(chip, core, *pieces[k])))

    def weigh_far(late, gate):
        rows = far[late]
        return weigh([r for r, _ in rows], [p for _, p in rows], after(far_codes, gate))

    far, far_cross = [[], []], {}
    partial = sum(near_s)
    masks = powers(groups)
    far_held.append(swap(after(held[1], first), "pts", far_mask))
    forward(0, partial)
    sums = [partial]
    here = [far_cross[c, 0] for c in range(1, chips) if (c, 0) in far_cross]
    for mask in masks[:-1]:
        sums.append(sums[-1] + swap(sums[-1], "pts", mask))
    sums.append(sums[-1] + swap(after(sums[-1], here), "pts", masks[-1]))
    column = sums[-1]
    for piece in held[2:]:
        far_held.append(swap(after(piece, first), "pts", far_mask))
    balance = call(functools.partial(balance_kernel, chips), [((1, slots), F32)], *near_w, column)
    steps = [balance]
    for k in range(1, len(pieces)):
        forward(k, column)
    for chip in range(chips):
        mine = parts[chips - 1 - chip]
        for k in mine[:-1]:
            pair(chip, k, column)
    far_got = [weigh_far(0, steps[0])]
    for k, mask in enumerate(masks[:-1]):
        came = swap(balance, "pts", mask)
        balance = balance + (after(came, far_got[0][0]) if mask == masks[-2] else came)
        steps.append(balance)
    for chip in range(chips):
        pair(chip, parts[chips - 1 - chip][-1], steps[-1])
    came = swap(balance, "pts", masks[-1])
    far_got.append(weigh_far(1, steps[-1]))
    balance = balance + after(came, far_got[1][0])
    far_w, far_x = zip(*[(w, x) for w, _, x in far_got])

    bits = powers(half_bit)
    orders = bit_orders(bits)
    cols = width // len(orders)
    m = half_bit // 2
    rows = [*near_x, *far_x]
    total_rows = sum(r.shape[0] for r in rows)
    part = pltpu.VMEM((max(share, LANES), cols), F32)
    def halves(blocks):
        n = len(blocks) // 2
        return [blocks[n:], blocks[:n]] if n else [blocks]

    early, late = [], []
    for r, (_, blocks) in enumerate(orders):
        first, *rest = halves(blocks[m:])
        early.append((r, first))
        late += [(r, blocks) for blocks in rest]
    kept = [(r, blocks[:m]) for r, (_, blocks) in enumerate(orders)]

    def shapes(wanted, dtype):
        return [((len(blocks), share, cols), dtype) for _, blocks in wanted]

    *firsts, assign = call(
        functools.partial(send_kernel, early, half_bit, len(near_w) + len(far_w)),
        shapes(early, BF16) + [((total_rows, slots // 2), BF16)],
        *near_w, *far_w, balance, *rows, scratch=[part],
    )
    got = list(call(
        functools.partial(keep_kernel, late + kept, half_bit), shapes(late, BF16) + shapes(kept, F32),
        assign, *rows, scratch=[part],
    ))
    seconds, keeps = got[: len(late)], got[len(late) :]
    terms = [[k] for k in keeps]
    sends = [[f] + seconds[r : r + 1] for r, f in enumerate(firsts)]
    for step in range(len(bits)):
        for r, (order, _) in enumerate(orders):
            came = [swap(a, "pts", order[step]) for a in sends[r]]
            n = came[0].shape[0]
            if len(came) == 1:
                terms[r].append(came[0])
                continue
            sends[r] = call(
                forward_kernel, [((max(n // 2, 1), share, cols), BF16)] * min(n, 2), keeps[r], came[0], vmem=8
            )
            sends[r] = list(sends[r]) if n > 1 else [sends[r]]
            if n > 1:
                keeps[r] = call(merge_kernel, [((n, share, cols), F32)], keeps[r], came[1], vmem=8)
                terms[r] = [keeps[r]]
            else:
                terms[r].append(came[1])
    flat = [t for route in terms for t in route]
    out = call(
        functools.partial(final_kernel, len(orders), len(terms[0])), [((share, width), BF16)], *flat, base, vmem=8
    )
    return out[None]


def solution(mesh):
    in_specs = (P(("pts", "own"), None), P("pts", None), P(), P(), P("own", None, None))
    out_specs = P("own", "pts", None)
    return jax.shard_map(local, mesh=mesh, in_specs=in_specs, out_specs=out_specs, check_vma=False)
```

```python
import functools

import jax
import jax.numpy as jnp
from jax import lax
from jax.experimental import pallas as pl
from jax.experimental.pallas import tpu as pltpu
from jax.sharding import PartitionSpec as P

F32 = jnp.float32
BF16 = jnp.bfloat16
I32 = jnp.int32
CORES = 2
ROWS = 16
LANES = 128
OWNER_SHIFT = 1 << 17
FIRST_SHIFT = 1 << 7


def down(value):
    return value // ROWS * ROWS


def up(value):
    return -(-value // ROWS) * ROWS


def iota(shape, dim):
    return lax.broadcasted_iota(I32, shape, dim)


def unit_rms(values):
    values = values.astype(F32)
    return values * lax.rsqrt(jnp.mean(values * values, axis=-1, keepdims=True) + 1e-06)


def windows(tok, owners):
    chips = owners // CORES
    full = 2 * tok // owners
    least = CORES * ((tok - full) // max(owners - 1, 1))
    starts = [down(j * least) for j in range(chips)]
    ends = [up(tok - (chips - 1 - j) * least) for j in range(chips)]
    wide = max(e - s for s, e in zip(starts, ends))
    starts = [min(s, tok - wide) for s in starts]
    starts = [min(s, tok - wide) for s in starts]
    soon = down(starts[min(1, chips - 1)] * 13 // 16)
    cuts = sorted({0, soon, tok} | {s + wide for s in starts})
    pieces = list(zip(cuts[:-1], cuts[1:]))
    parts = [[k for k, (lo, hi) in enumerate(pieces) if lo < s + wide and s < hi] for s in starts]
    return starts, wide, pieces, parts


def to_col(row):
    n = row.shape[1]
    return jnp.sum(jnp.where(iota((n, n), 0) == iota((n, n), 1), row, 0.0), axis=1, keepdims=True)


def to_row(col):
    n = col.shape[0]
    return jnp.sum(jnp.where(iota((n, n), 0) == iota((n, n), 1), col, 0.0), axis=0, keepdims=True)


def owner_codes(owner_ref, count_ref):
    owner = owner_ref[...].astype(F32)
    count = count_ref[...].astype(F32)
    n = owner.shape[1]
    earlier = (to_col(owner) == owner) & (iota((n, n), 0) < iota((n, n), 1))
    first = jnp.sum(jnp.where(earlier, to_col(count), 0.0), axis=0, keepdims=True)
    return owner * OWNER_SHIFT + first * FIRST_SHIFT + count


def code_and_key(parent_row, code_row, chip, chips):
    parent = to_col(parent_row.astype(F32)).astype(I32)
    tok = parent.shape[0]
    n = code_row.shape[1]
    code = jnp.sum(jnp.where(parent == iota((tok, n), 1), code_row, 0.0), axis=1, keepdims=True)
    owner = code.astype(I32) // OWNER_SHIFT
    order = (chips - 1) - ((owner // CORES) ^ chip)
    key = (order * tok + iota((tok, 1), 0)).astype(F32)
    return code, key


def fetch(pairs, sems):
    copies = [pltpu.make_async_copy(src, dst, sems.at[k]) for k, (src, dst) in enumerate(pairs)]
    for copy in copies:
        copy.start()
    return copies


def sort_kernel(chips, ranges, *refs):
    points_ref, parents_ref, owner_ref, count_ref = refs[:4]
    out_refs, (parents, table, points, owner, count, sems) = refs[4:-6], refs[-6:]
    copies = fetch(
        [(points_ref, points), (parents_ref, parents), (owner_ref, owner), (count_ref, count)], sems
    )
    me = lax.axis_index("own")
    tok = points.shape[0]
    for copy in copies[1:]:
        copy.wait()
    code_row = owner_codes(owner, count)
    table[...] = code_row
    parent = parents[:, pl.ds(pl.multiple_of(me * tok, tok), tok)]
    code, key = code_and_key(parent, code_row, me // CORES, chips)
    key_row = to_row(key)
    place = jnp.sum(jnp.where(key < key_row, 1.0, 0.0), axis=0, keepdims=True).astype(I32)
    pick = jnp.where(iota((tok, tok), 0) == place, 1.0, 0.0).astype(BF16)
    copies[0].wait()
    unit = unit_rms(points[...]).astype(BF16)
    ordered = jnp.dot(pick, unit, preferred_element_type=F32).astype(BF16)
    for (lo, hi), out_ref in zip(ranges, out_refs):
        out_ref[...] = ordered[lo:hi]


def codes_kernel(chips, starts, tok, wide, parents, table, out_ref):
    me = lax.axis_index("own")
    code_row = table[...]
    total = out_ref.shape[1]
    out = jnp.zeros((1, total), F32)
    for rel in range(total // wide):
        parent = parents[:, pl.ds(pl.multiple_of((me ^ rel) * tok, tok), tok)]
        code, key = code_and_key(parent, code_row, (me ^ rel) // CORES, chips)
        place = jnp.sum(jnp.where(to_row(key) < key, 1.0, 0.0), axis=1, keepdims=True).astype(I32)
        inside = iota((tok, total), 1) - rel * wide
        hit = (inside >= 0) & (inside < wide) & (place == inside + starts[chips - 1 - rel // CORES])
        out = out + jnp.sum(jnp.where(hit, code, 0.0), axis=0, keepdims=True)
    out_ref[...] = out


def cent_kernel(in_ref, out_ref, base_ref):
    out_ref[...] = unit_rms(in_ref[...]).astype(BF16)
    share = base_ref.shape[0]
    base_ref[...] = out_ref[pl.ds(pl.multiple_of(lax.axis_index("pts") * share, share), share), :]


def bounds_kernel(places, slots, codes_ref, low_ref, high_ref):
    me = lax.axis_index("own")
    total = codes_ref.shape[1]
    at = 0
    for place, _, size in places:
        part = slice(at, at + size)
        at += size
        hit = iota((size, total), 1) == iota((size, total), 0) + place
        code = jnp.sum(jnp.where(hit, codes_ref[...], 0.0), axis=1, keepdims=True).astype(I32)
        first = (code % OWNER_SHIFT) // FIRST_SHIFT
        low = jnp.where(code // OWNER_SHIFT == me, first, slots)
        low_ref[part, :] = low
        high_ref[part, :] = low + code % FIRST_SHIFT


def coded_kernel(places, tile, half_bit, *refs):
    codes_ref, cent_ref, low_ref, high_ref = refs[-7], refs[-6], refs[-2], refs[-1]
    bounds_kernel(places, cent_ref.shape[0], codes_ref, low_ref, high_ref)
    weights_kernel(places, tile, half_bit, *refs[:-7], low_ref, high_ref, *refs[-6:-2])


def weights_kernel(places, tile, half_bit, *refs):
    row_refs, (low_ref, high_ref, cent_ref, w_ref, sum_ref, rows_ref) = refs[:-6], refs[-6:]
    slots, width = cent_ref.shape
    at = 0
    for row_ref, (_, skip, size) in zip(row_refs, places):
        rows_ref[at : at + size, :] = row_ref[skip : skip + size, :]
        at += size
    span = w_ref.shape[1]
    base = span_start(half_bit, slots, span)

    def step(i, carry):
        at = pl.multiple_of(i * tile, tile)
        cent = cent_ref[pl.ds(pl.multiple_of(base + at, LANES), tile), :]
        scores = lax.dot_general(rows_ref[...], cent, (((1,), (1,)), ((), ())), preferred_element_type=F32)
        slot = iota(scores.shape, 1) + (base + at)
        live = (slot >= low_ref[...]) & (slot < high_ref[...])
        w = jnp.where(live, jnp.exp(scores * (1.0 / (width * 0.05))), 0.0)
        w_ref[:, pl.ds(at, tile)] = w
        sum_ref[:, pl.ds(at, tile)] = jnp.sum(w, axis=0, keepdims=True)
        return carry

    lax.fori_loop(0, span // tile, step, 0, unroll=True)


def span_start(half_bit, slots, span):
    return (lax.axis_index("pts") // half_bit) % 2 * (slots - span)


def inverse(values):
    return jnp.where(values > 0.0, 1.0 / jnp.where(values > 0.0, values, 1.0), 0.0)


def balance_kernel(n, *refs):
    w_refs, col_ref, out_ref = refs[:n], refs[n], refs[n + 1]
    scale = inverse(col_ref[...])
    total = jnp.zeros_like(scale)
    for w_ref in w_refs:
        rows = w_ref.shape[0]
        for at in range(0, rows, ROWS * 2):
            w = w_ref[at : at + ROWS * 2, :]
            row = jnp.sum(w * scale, axis=1, keepdims=True)
            total = total + jnp.sum(w * inverse(row), axis=0, keepdims=True)
    out_ref[...] = total


def assign_kernel(half_bit, *refs):
    w_refs, (t_ref, assign_ref) = refs[:-2], refs[-2:]
    slots, half = t_ref.shape[1], assign_ref.shape[1]
    upper = (lax.axis_index("pts") // half_bit) % 2
    part = inverse(t_ref[:, pl.ds(pl.multiple_of(upper * half, half), half)])
    at = 0
    for w_ref in w_refs:
        span = w_ref.shape[1]
        base = span_start(half_bit, slots, span)
        scale = inverse(t_ref[:, pl.ds(pl.multiple_of(base, LANES), span)])
        columns = pl.ds(pl.multiple_of(upper * (span - half), LANES), half)
        for lo in range(0, w_ref.shape[0], ROWS * 2):
            row = inverse(jnp.sum(w_ref[lo : lo + ROWS * 2, :] * scale, axis=1, keepdims=True))
            mine = w_ref[lo : lo + ROWS * 2, columns] * part
            assign_ref[at : at + ROWS * 2, :] = (mine * row).astype(BF16)
            at += ROWS * 2


def move_kernel(wanted, half_bit, assign_ref, row_refs, out_refs, part_ref):
    low = lax.axis_index("pts") % half_bit
    for (which, order), out_ref in zip(wanted, out_refs):
        share, cols = out_ref.shape[1:]
        block = part_ref.shape[0]
        lanes = slice(which * cols, (which + 1) * cols)
        for k, rel in enumerate(order):
            start = (low ^ rel) * share
            columns = pl.ds(pl.multiple_of(start // block * block, block), block)
            moved, at = 0.0, 0
            for r in row_refs:
                a = assign_ref[at : at + r.shape[0], columns]
                moved = moved + lax.dot_general(
                    a, r[:, lanes], (((0,), (0,)), ((), ())), preferred_element_type=F32
                )
                at += r.shape[0]
            if share < block:
                part_ref[...] = moved
                moved = part_ref[pl.ds(pl.multiple_of(start % block, share), share), :]
            out_ref[k] = moved.astype(out_ref.dtype)


def send_kernel(wanted, half_bit, nw, *refs):
    n = len(wanted)
    row_refs, out_refs = refs[nw + 1 : -n - 2], refs[-n - 2 : -2]
    assign_ref, part_ref = refs[-2:]
    assign_kernel(half_bit, *refs[: nw + 1], assign_ref)
    move_kernel(wanted, half_bit, assign_ref, row_refs, out_refs, part_ref)


def keep_kernel(wanted, half_bit, *refs):
    n = len(wanted)
    move_kernel(wanted, half_bit, refs[0], refs[1 : -n - 1], refs[-n - 1 : -1], refs[-1])


def forward_kernel(keep_ref, came_ref, *out_refs):
    n = came_ref.shape[0]
    total = (keep_ref[n:] + came_ref[...].astype(F32)).astype(BF16)
    at = n
    for out_ref in out_refs:
        at -= out_ref.shape[0]
        out_ref[...] = total[at : at + out_ref.shape[0]]


def merge_kernel(keep_ref, came_ref, out_ref):
    out_ref[...] = keep_ref[: came_ref.shape[0]] + came_ref[...].astype(F32)


def final_kernel(nroute, nterm, *refs):
    base_ref, out_ref = refs[nroute * nterm], refs[nroute * nterm + 1]
    parts = []
    for which in range(nroute):
        total = 0.0
        for ref in refs[which * nterm : (which + 1) * nterm]:
            total = total + ref[0].astype(F32)
        parts.append(total)
    moved = jnp.concatenate(parts, axis=1)
    out_ref[...] = unit_rms(base_ref[...].astype(F32) + 8.0 * moved).astype(BF16)


def call(kernel, outs, *args, scratch=(), flops=0, vmem=16, where=pltpu.VMEM):
    shapes = [jax.ShapeDtypeStruct(s, d) for s, d in outs]
    size = sum(a.size * a.dtype.itemsize for a in args) + sum(s.size * s.dtype.itemsize for s in shapes)
    got = pl.pallas_call(
        kernel,
        out_shape=shapes,
        in_specs=[pl.BlockSpec(memory_space=where)] * len(args),
        out_specs=[pl.BlockSpec(memory_space=pltpu.VMEM)] * len(shapes),
        scratch_shapes=list(scratch),
        compiler_params=pltpu.CompilerParams(vmem_limit_bytes=vmem << 20),
        cost_estimate=pl.CostEstimate(flops=flops, bytes_accessed=0, transcendentals=0),
    )(*args)
    return got[0] if len(shapes) == 1 else got


def after(values, gate):
    return lax.optimization_barrier((values, gate))[0]


def swap(values, axis, bit):
    return lax.ppermute(values, axis, [(i, i ^ bit) for i in range(lax.axis_size(axis))])


def powers(end):
    return [1 << k for k in range(end.bit_length() - 1)]


def bit_orders(bits):
    orders = []
    for k in range(len(bits)):
        order = bits[k:] + bits[:k]
        blocks = [0]
        for bit in reversed(order):
            blocks = blocks + [b | bit for b in blocks]
        orders.append((order, blocks))
    return orders


def local(points, parent_of, owner_of, child_count, centroids):
    owners, groups = lax.axis_size("own"), lax.axis_size("pts")
    chips = owners // CORES
    tok, width = points.shape
    slots = centroids.shape[1]
    share = slots // groups
    starts, wide, pieces, parts = windows(tok, owners)
    parents = parent_of.T
    table = [owner_of.reshape(1, -1), child_count.reshape(1, -1)]
    half_bit = groups // 2
    far_mask = half_bit | half_bit >> 1

    ranges = pieces + [(s, s + wide) for s in starts]
    *ordered, parents, codes = call(
        functools.partial(sort_kernel, chips, ranges),
        [((hi - lo, width), BF16) for lo, hi in ranges] + [(parents.shape, I32), (table[0].shape, F32)],
        points, parents, *table,
        scratch=[
            pltpu.VMEM((tok, width), BF16), *[pltpu.VMEM(a.shape, I32) for a in table],
            pltpu.SemaphoreType.DMA((4,)),
        ],
        where=pl.ANY, vmem=62,
    )
    held, whole = ordered[: len(pieces)], ordered[len(pieces) :]

    def place(chip, core, lo, hi):
        start = starts[chips - 1 - chip]
        first, last = max(lo, start), min(hi, start + wide)
        return (chip * CORES + core) * wide + first - start, first - lo, last - first

    def weigh(rows, places, codes, span=slots, bounds=None):
        count = sum(size for _, _, size in places)
        column = pltpu.VMEM((count, 1), I32)
        return call(
            functools.partial(weights_kernel if bounds else coded_kernel, places, 256 if span % 256 == 0 else span, half_bit),
            [((count, span), F32), ((1, span), F32), ((count, width), BF16)],
            *rows, *(bounds or [codes]), cent, scratch=[] if bounds else [column, column],
        )

    near = [whole[-1]] + [swap(whole[chips - 1 - chip], "own", chip * CORES) for chip in range(1, chips)]
    far_held = [swap(held[0], "pts", far_mask)]
    codes = call(
        functools.partial(codes_kernel, chips, starts, tok, wide), [((1, owners * wide), F32)], parents, codes,
        vmem=4,
    )
    cent, base = call(cent_kernel, [((slots, width), BF16), ((share, width), BF16)], centroids[0])

    far_codes = swap(codes, "pts", far_mask)

    def weigh_near(chip, rows, codes):
        start = starts[chips - 1 - chip]
        return weigh((rows, swap(rows, "own", 1)), [place(chip, c, start, start + wide) for c in range(CORES)], codes)

    near_got = [weigh_near(0, near[0], codes)]
    first = near_got[0][1]
    for chip in range(1, chips):
        near_got.append(weigh_near(chip, after(near[chip], (first, far_held[0], far_codes)), codes))
    near_w, near_s, near_x = zip(*near_got)

    def forward(k, gate):
        for chip in range(1, chips):
            if k in parts[chips - 1 - chip]:
                far_cross[chip, k] = swap(after(far_held[k], gate), "own", chip * CORES)

    def pair(chip, k, gate):
        rows = after(far_cross[chip, k] if chip else far_held[k], gate)
        for core, r in enumerate((rows, swap(rows, "own", 1))):
            far[int(k == parts[chips - 1 - chip][-1])].append((r, place(chip, core, *pieces[k])))

    def weigh_far(late, gate, bounds=None):
        rows, places = zip(*far[late])
        return weigh(rows, places, after(far_codes, gate), min(slots // 2 + LANES, slots), bounds)

    far, far_cross = [[], []], {}
    partial = sum(near_s)
    masks = powers(groups)
    far_held.append(swap(after(held[1], first), "pts", far_mask))
    forward(0, partial)
    sums = [partial]
    here = [far_cross[c, 0] for c in range(1, chips) if (c, 0) in far_cross]
    for mask in masks[:-1]:
        sums.append(sums[-1] + swap(sums[-1], "pts", mask))
    sums.append(sums[-1] + swap(after(sums[-1], here), "pts", masks[-1]))
    column = sums[-1]
    for piece in held[2:]:
        far_held.append(swap(after(piece, first), "pts", far_mask))
    balance = call(functools.partial(balance_kernel, chips), [((1, slots), F32)], *near_w, column)
    steps = [balance]
    for k in range(1, len(pieces)):
        forward(k, column)
    for chip in range(chips):
        mine = parts[chips - 1 - chip]
        for k in mine[:-1]:
            pair(chip, k, column)
    late = [place(chip, c, *pieces[parts[chips - 1 - chip][-1]]) for chip in range(chips) for c in range(CORES)]
    count = sum(size for _, _, size in late)
    bounds = call(
        functools.partial(bounds_kernel, late, slots), [((count, 1), I32)] * 2, after(far_codes, steps[0]), vmem=4
    )
    far_got = [weigh_far(0, bounds[0])]
    for k, mask in enumerate(masks[:-1]):
        came = swap(balance, "pts", mask)
        balance = balance + (after(came, far_got[0][0]) if mask == masks[-2] else came)
        steps.append(balance)
    for chip in range(chips):
        pair(chip, parts[chips - 1 - chip][-1], steps[-1])
    came = swap(balance, "pts", masks[-1])
    far_got.append(weigh_far(1, steps[-1], list(bounds)))
    balance = balance + after(came, far_got[1][0])
    far_w, far_x = zip(*[(w, x) for w, _, x in far_got])

    bits = powers(half_bit)
    orders = bit_orders(bits)
    cols = width // len(orders)
    m = half_bit // 2
    rows = [*near_x, *far_x]
    total_rows = sum(r.shape[0] for r in rows)
    part = pltpu.VMEM((max(share, LANES), cols), F32)
    def halves(blocks):
        n = len(blocks) // 2
        return [blocks[n:], blocks[:n]] if n else [blocks]

    early, late = [], []
    for r, (_, blocks) in enumerate(orders):
        first, *rest = halves(blocks[m:])
        early.append((r, first))
        late += [(r, blocks) for blocks in rest]
    kept = [(r, blocks[:m]) for r, (_, blocks) in enumerate(orders)]

    def shapes(wanted, dtype):
        return [((len(blocks), share, cols), dtype) for _, blocks in wanted]

    *firsts, assign = call(
        functools.partial(send_kernel, early, half_bit, len(near_w) + len(far_w)),
        shapes(early, BF16) + [((total_rows, slots // 2), BF16)],
        *near_w, *far_w, balance, *rows, scratch=[part],
    )
    got = list(call(
        functools.partial(keep_kernel, late + kept, half_bit), shapes(late, BF16) + shapes(kept, F32),
        assign, *rows, scratch=[part],
    ))
    seconds, keeps = got[: len(late)], got[len(late) :]
    terms = [[k] for k in keeps]
    sends = [[f] + seconds[r : r + 1] for r, f in enumerate(firsts)]
    for step in range(len(bits)):
        for r, (order, _) in enumerate(orders):
            came = [swap(a, "pts", order[step]) for a in sends[r]]
            n = came[0].shape[0]
            if len(came) == 1:
                terms[r].append(came[0])
                continue
            sends[r] = call(
                forward_kernel, [((max(n // 2, 1), share, cols), BF16)] * min(n, 2), keeps[r], came[0], vmem=8
            )
            sends[r] = list(sends[r]) if n > 1 else [sends[r]]
            if n > 1:
                keeps[r] = call(merge_kernel, [((n, share, cols), F32)], keeps[r], came[1], vmem=8)
                terms[r] = [keeps[r]]
            else:
                terms[r].append(came[1])
    flat = [t for route in terms for t in route]
    out = call(
        functools.partial(final_kernel, len(orders), len(terms[0])), [((share, width), BF16)], *flat, base, vmem=8
    )
    return out[None]


def solution(mesh):
    in_specs = (P(("pts", "own"), None), P("pts", None), P(), P(), P("own", None, None))
    out_specs = P("own", "pts", None)
    return jax.shard_map(local, mesh=mesh, in_specs=in_specs, out_specs=out_specs, check_vma=False)
```

```python
import functools

import jax
import jax.numpy as jnp
from jax import lax
from jax.experimental import pallas as pl
from jax.experimental.pallas import tpu as pltpu
from jax.sharding import PartitionSpec as P

F32 = jnp.float32
BF16 = jnp.bfloat16
I32 = jnp.int32
CORES = 2
ROWS = 16
LANES = 128
OWNER_SHIFT = 1 << 17
FIRST_SHIFT = 1 << 7


def down(value):
    return value // ROWS * ROWS


def up(value):
    return -(-value // ROWS) * ROWS


def iota(shape, dim):
    return lax.broadcasted_iota(I32, shape, dim)


def unit_rms(values):
    values = values.astype(F32)
    return values * lax.rsqrt(jnp.mean(values * values, axis=-1, keepdims=True) + 1e-06)


def windows(tok, owners):
    chips = owners // CORES
    full = 2 * tok // owners
    least = CORES * ((tok - full) // max(owners - 1, 1))
    starts = [down(j * least) for j in range(chips)]
    ends = [up(tok - (chips - 1 - j) * least) for j in range(chips)]
    wide = max(e - s for s, e in zip(starts, ends))
    starts = [min(s, tok - wide) for s in starts]
    starts = [min(s, tok - wide) for s in starts]
    soon = starts[min(1, chips - 1)]
    cuts = sorted({0, soon, tok} | {s + wide for s in starts})
    pieces = list(zip(cuts[:-1], cuts[1:]))
    parts = [[k for k, (lo, hi) in enumerate(pieces) if lo < s + wide and s < hi] for s in starts]
    return starts, wide, pieces, parts


def to_col(row):
    n = row.shape[1]
    return jnp.sum(jnp.where(iota((n, n), 0) == iota((n, n), 1), row, 0.0), axis=1, keepdims=True)


def to_row(col):
    n = col.shape[0]
    return jnp.sum(jnp.where(iota((n, n), 0) == iota((n, n), 1), col, 0.0), axis=0, keepdims=True)


def owner_codes(owner_ref, count_ref):
    owner = owner_ref[...].astype(F32)
    count = count_ref[...].astype(F32)
    n = owner.shape[1]
    earlier = (to_col(owner) == owner) & (iota((n, n), 0) < iota((n, n), 1))
    first = jnp.sum(jnp.where(earlier, to_col(count), 0.0), axis=0, keepdims=True)
    return owner * OWNER_SHIFT + first * FIRST_SHIFT + count


def code_and_key(parent_row, code_row, chip, chips):
    parent = to_col(parent_row.astype(F32)).astype(I32)
    tok = parent.shape[0]
    n = code_row.shape[1]
    code = jnp.sum(jnp.where(parent == iota((tok, n), 1), code_row, 0.0), axis=1, keepdims=True)
    owner = code.astype(I32) // OWNER_SHIFT
    order = (chips - 1) - ((owner // CORES) ^ chip)
    key = (order * tok + iota((tok, 1), 0)).astype(F32)
    return code, key


def fetch(pairs, sems):
    copies = [pltpu.make_async_copy(src, dst, sems.at[k]) for k, (src, dst) in enumerate(pairs)]
    for copy in copies:
        copy.start()
    return copies


def sort_kernel(chips, ranges, *refs):
    points_ref, parents_ref, owner_ref, count_ref = refs[:4]
    out_refs, (parents, table, points, owner, count, sems) = refs[4:-6], refs[-6:]
    copies = fetch(
        [(points_ref, points), (parents_ref, parents), (owner_ref, owner), (count_ref, count)], sems
    )
    me = lax.axis_index("own")
    tok = points.shape[0]
    for copy in copies[1:]:
        copy.wait()
    code_row = owner_codes(owner, count)
    table[...] = code_row
    parent = parents[:, pl.ds(pl.multiple_of(me * tok, tok), tok)]
    code, key = code_and_key(parent, code_row, me // CORES, chips)
    key_row = to_row(key)
    place = jnp.sum(jnp.where(key < key_row, 1.0, 0.0), axis=0, keepdims=True).astype(I32)
    pick = jnp.where(iota((tok, tok), 0) == place, 1.0, 0.0).astype(BF16)
    copies[0].wait()
    unit = unit_rms(points[...]).astype(BF16)
    ordered = jnp.dot(pick, unit, preferred_element_type=F32).astype(BF16)
    for (lo, hi), out_ref in zip(ranges, out_refs):
        out_ref[...] = ordered[lo:hi]


def codes_kernel(chips, starts, tok, wide, parents, table, out_ref):
    me = lax.axis_index("own")
    code_row = table[...]
    total = out_ref.shape[1]
    out = jnp.zeros((1, total), F32)
    for rel in range(total // wide):
        parent = parents[:, pl.ds(pl.multiple_of((me ^ rel) * tok, tok), tok)]
        code, key = code_and_key(parent, code_row, (me ^ rel) // CORES, chips)
        place = jnp.sum(jnp.where(to_row(key) < key, 1.0, 0.0), axis=1, keepdims=True).astype(I32)
        inside = iota((tok, total), 1) - rel * wide
        hit = (inside >= 0) & (inside < wide) & (place == inside + starts[chips - 1 - rel // CORES])
        out = out + jnp.sum(jnp.where(hit, code, 0.0), axis=0, keepdims=True)
    out_ref[...] = out


def cent_kernel(in_ref, out_ref, base_ref):
    out_ref[...] = unit_rms(in_ref[...]).astype(BF16)
    share = base_ref.shape[0]
    base_ref[...] = out_ref[pl.ds(pl.multiple_of(lax.axis_index("pts") * share, share), share), :]


def bounds_kernel(places, slots, codes_ref, low_ref, high_ref):
    me = lax.axis_index("own")
    total = codes_ref.shape[1]
    at = 0
    for place, _, size in places:
        part = slice(at, at + size)
        at += size
        hit = iota((size, total), 1) == iota((size, total), 0) + place
        code = jnp.sum(jnp.where(hit, codes_ref[...], 0.0), axis=1, keepdims=True).astype(I32)
        first = (code % OWNER_SHIFT) // FIRST_SHIFT
        low = jnp.where(code // OWNER_SHIFT == me, first, slots)
        low_ref[part, :] = low
        high_ref[part, :] = low + code % FIRST_SHIFT


def coded_kernel(places, tile, half_bit, *refs):
    codes_ref, cent_ref, low_ref, high_ref = refs[-7], refs[-6], refs[-2], refs[-1]
    bounds_kernel(places, cent_ref.shape[0], codes_ref, low_ref, high_ref)
    weights_kernel(places, tile, half_bit, *refs[:-7], low_ref, high_ref, *refs[-6:-2])


def weights_kernel(places, tile, half_bit, *refs):
    row_refs, (low_ref, high_ref, cent_ref, w_ref, sum_ref, rows_ref) = refs[:-6], refs[-6:]
    slots, width = cent_ref.shape
    at = 0
    for row_ref, (_, skip, size) in zip(row_refs, places):
        rows_ref[at : at + size, :] = row_ref[skip : skip + size, :]
        at += size
    span = w_ref.shape[1]
    base = span_start(half_bit, slots, span)

    def step(i, carry):
        at = pl.multiple_of(i * tile, tile)
        cent = cent_ref[pl.ds(pl.multiple_of(base + at, LANES), tile), :]
        scores = lax.dot_general(rows_ref[...], cent, (((1,), (1,)), ((), ())), preferred_element_type=F32)
        slot = iota(scores.shape, 1) + (base + at)
        live = (slot >= low_ref[...]) & (slot < high_ref[...])
        w = jnp.where(live, jnp.exp(scores * (1.0 / (width * 0.05))), 0.0)
        w_ref[:, pl.ds(at, tile)] = w
        sum_ref[:, pl.ds(at, tile)] = jnp.sum(w, axis=0, keepdims=True)
        return carry

    lax.fori_loop(0, span // tile, step, 0, unroll=True)


def span_start(half_bit, slots, span):
    return (lax.axis_index("pts") // half_bit) % 2 * (slots - span)


def inverse(values):
    return jnp.where(values > 0.0, 1.0 / jnp.where(values > 0.0, values, 1.0), 0.0)


def balance_kernel(n, *refs):
    w_refs, col_ref, out_ref = refs[:n], refs[n], refs[n + 1]
    scale = inverse(col_ref[...])
    total = jnp.zeros_like(scale)
    for w_ref in w_refs:
        rows = w_ref.shape[0]
        for at in range(0, rows, ROWS * 2):
            w = w_ref[at : at + ROWS * 2, :]
            row = jnp.sum(w * scale, axis=1, keepdims=True)
            total = total + jnp.sum(w * inverse(row), axis=0, keepdims=True)
    out_ref[...] = total


def assign_kernel(half_bit, *refs):
    w_refs, (t_ref, assign_ref) = refs[:-2], refs[-2:]
    slots, half = t_ref.shape[1], assign_ref.shape[1]
    upper = (lax.axis_index("pts") // half_bit) % 2
    part = inverse(t_ref[:, pl.ds(pl.multiple_of(upper * half, half), half)])
    at = 0
    for w_ref in w_refs:
        span = w_ref.shape[1]
        base = span_start(half_bit, slots, span)
        scale = inverse(t_ref[:, pl.ds(pl.multiple_of(base, LANES), span)])
        columns = pl.ds(pl.multiple_of(upper * (span - half), LANES), half)
        for lo in range(0, w_ref.shape[0], ROWS * 2):
            row = inverse(jnp.sum(w_ref[lo : lo + ROWS * 2, :] * scale, axis=1, keepdims=True))
            mine = w_ref[lo : lo + ROWS * 2, columns] * part
            assign_ref[at : at + ROWS * 2, :] = (mine * row).astype(BF16)
            at += ROWS * 2


def move_kernel(wanted, half_bit, assign_ref, row_refs, out_refs, part_ref):
    low = lax.axis_index("pts") % half_bit
    for (which, order), out_ref in zip(wanted, out_refs):
        share, cols = out_ref.shape[1:]
        block = part_ref.shape[0]
        lanes = slice(which * cols, (which + 1) * cols)
        for k, rel in enumerate(order):
            start = (low ^ rel) * share
            columns = pl.ds(pl.multiple_of(start // block * block, block), block)
            moved, at = 0.0, 0
            for r in row_refs:
                a = assign_ref[at : at + r.shape[0], columns]
                moved = moved + lax.dot_general(
                    a, r[:, lanes], (((0,), (0,)), ((), ())), preferred_element_type=F32
                )
                at += r.shape[0]
            if share < block:
                part_ref[...] = moved
                moved = part_ref[pl.ds(pl.multiple_of(start % block, share), share), :]
            out_ref[k] = moved.astype(out_ref.dtype)


def send_kernel(wanted, half_bit, nw, *refs):
    n = len(wanted)
    row_refs, out_refs = refs[nw + 1 : -n - 2], refs[-n - 2 : -2]
    assign_ref, part_ref = refs[-2:]
    assign_kernel(half_bit, *refs[: nw + 1], assign_ref)
    move_kernel(wanted, half_bit, assign_ref, row_refs, out_refs, part_ref)


def keep_kernel(wanted, half_bit, *refs):
    n = len(wanted)
    move_kernel(wanted, half_bit, refs[0], refs[1 : -n - 1], refs[-n - 1 : -1], refs[-1])


def forward_kernel(keep_ref, came_ref, *out_refs):
    n = came_ref.shape[0]
    total = (keep_ref[n:] + came_ref[...].astype(F32)).astype(BF16)
    at = n
    for out_ref in out_refs:
        at -= out_ref.shape[0]
        out_ref[...] = total[at : at + out_ref.shape[0]]


def merge_kernel(keep_ref, came_ref, out_ref):
    out_ref[...] = keep_ref[: came_ref.shape[0]] + came_ref[...].astype(F32)


def final_kernel(nroute, nterm, *refs):
    base_ref, out_ref = refs[nroute * nterm], refs[nroute * nterm + 1]
    parts = []
    for which in range(nroute):
        total = 0.0
        for ref in refs[which * nterm : (which + 1) * nterm]:
            total = total + ref[0].astype(F32)
        parts.append(total)
    moved = jnp.concatenate(parts, axis=1)
    out_ref[...] = unit_rms(base_ref[...].astype(F32) + 8.0 * moved).astype(BF16)


def call(kernel, outs, *args, scratch=(), flops=0, vmem=16, where=pltpu.VMEM):
    shapes = [jax.ShapeDtypeStruct(s, d) for s, d in outs]
    size = sum(a.size * a.dtype.itemsize for a in args) + sum(s.size * s.dtype.itemsize for s in shapes)
    got = pl.pallas_call(
        kernel,
        out_shape=shapes,
        in_specs=[pl.BlockSpec(memory_space=where)] * len(args),
        out_specs=[pl.BlockSpec(memory_space=pltpu.VMEM)] * len(shapes),
        scratch_shapes=list(scratch),
        compiler_params=pltpu.CompilerParams(vmem_limit_bytes=vmem << 20),
        cost_estimate=pl.CostEstimate(flops=flops, bytes_accessed=0, transcendentals=0),
    )(*args)
    return got[0] if len(shapes) == 1 else got


def after(values, gate):
    return lax.optimization_barrier((values, gate))[0]


def swap(values, axis, bit):
    return lax.ppermute(values, axis, [(i, i ^ bit) for i in range(lax.axis_size(axis))])


def powers(end):
    return [1 << k for k in range(end.bit_length() - 1)]


def bit_orders(bits):
    orders = []
    for k in range(len(bits)):
        order = bits[k:] + bits[:k]
        blocks = [0]
        for bit in reversed(order):
            blocks = blocks + [b | bit for b in blocks]
        orders.append((order, blocks))
    return orders


def local(points, parent_of, owner_of, child_count, centroids):
    owners, groups = lax.axis_size("own"), lax.axis_size("pts")
    chips = owners // CORES
    tok, width = points.shape
    slots = centroids.shape[1]
    share = slots // groups
    starts, wide, pieces, parts = windows(tok, owners)
    parents = parent_of.T
    table = [owner_of.reshape(1, -1), child_count.reshape(1, -1)]
    half_bit = groups // 2
    far_mask = half_bit | half_bit >> 1

    ranges = pieces + [(s, s + wide) for s in starts]
    *ordered, parents, codes = call(
        functools.partial(sort_kernel, chips, ranges),
        [((hi - lo, width), BF16) for lo, hi in ranges] + [(parents.shape, I32), (table[0].shape, F32)],
        points, parents, *table,
        scratch=[
            pltpu.VMEM((tok, width), BF16), *[pltpu.VMEM(a.shape, I32) for a in table],
            pltpu.SemaphoreType.DMA((4,)),
        ],
        where=pl.ANY, vmem=62,
    )
    held, whole = ordered[: len(pieces)], ordered[len(pieces) :]

    def place(chip, core, lo, hi):
        start = starts[chips - 1 - chip]
        first, last = max(lo, start), min(hi, start + wide)
        return (chip * CORES + core) * wide + first - start, first - lo, last - first

    def weigh(rows, places, codes, span=slots, bounds=None):
        count = sum(size for _, _, size in places)
        column = pltpu.VMEM((count, 1), I32)
        return call(
            functools.partial(weights_kernel if bounds else coded_kernel, places, 256 if span % 256 == 0 else span, half_bit),
            [((count, span), F32), ((1, span), F32), ((count, width), BF16)],
            *rows, *(bounds or [codes]), cent, scratch=[] if bounds else [column, column],
        )

    near = [whole[-1]] + [swap(whole[chips - 1 - chip], "own", chip * CORES) for chip in range(1, chips)]
    far_held = [swap(held[0], "pts", far_mask)]
    codes = call(
        functools.partial(codes_kernel, chips, starts, tok, wide), [((1, owners * wide), F32)], parents, codes,
        vmem=4,
    )
    cent, base = call(cent_kernel, [((slots, width), BF16), ((share, width), BF16)], centroids[0])

    far_codes = swap(codes, "pts", far_mask)

    def weigh_near(chip, rows, codes):
        start = starts[chips - 1 - chip]
        return weigh((rows, swap(rows, "own", 1)), [place(chip, c, start, start + wide) for c in range(CORES)], codes)

    near_got = [weigh_near(0, near[0], codes)]
    first = near_got[0][1]
    for chip in range(1, chips):
        near_got.append(weigh_near(chip, after(near[chip], (first, far_held[0], far_codes)), codes))
    near_w, near_s, near_x = zip(*near_got)

    def forward(k, gate):
        for chip in range(1, chips):
            if k in parts[chips - 1 - chip]:
                far_cross[chip, k] = swap(after(far_held[k], gate), "own", chip * CORES)

    def pair(chip, k, gate):
        rows = after(far_cross[chip, k] if chip else far_held[k], gate)
        for core, r in enumerate((rows, swap(rows, "own", 1))):
            far[int(k == parts[chips - 1 - chip][-1])].append((r, place(chip, core, *pieces[k])))

    def weigh_far(late, gate, bounds=None):
        rows, places = zip(*far[late])
        return weigh(rows, places, after(far_codes, gate), min(slots // 2 + LANES, slots), bounds)

    far, far_cross = [[], []], {}
    partial = sum(near_s)
    masks = powers(groups)
    far_held.append(swap(after(held[1], first), "pts", far_mask))
    forward(0, partial)
    sums = [partial]
    here = [far_cross[c, 0] for c in range(1, chips) if (c, 0) in far_cross]
    for mask in masks[:-1]:
        sums.append(sums[-1] + swap(sums[-1], "pts", mask))
    sums.append(sums[-1] + swap(after(sums[-1], here), "pts", masks[-1]))
    column = sums[-1]
    for piece in held[2:]:
        far_held.append(swap(after(piece, first), "pts", far_mask))
    balance = call(functools.partial(balance_kernel, chips), [((1, slots), F32)], *near_w, column)
    steps = [balance]
    for k in range(1, len(pieces)):
        forward(k, column)
    for chip in range(chips):
        mine = parts[chips - 1 - chip]
        for k in mine[:-1]:
            pair(chip, k, column)
    late = [place(chip, c, *pieces[parts[chips - 1 - chip][-1]]) for chip in range(chips) for c in range(CORES)]
    count = sum(size for _, _, size in late)
    bounds = call(
        functools.partial(bounds_kernel, late, slots), [((count, 1), I32)] * 2, after(far_codes, steps[0]), vmem=4
    )
    far_got = [weigh_far(0, bounds[0])]
    for k, mask in enumerate(masks[:-1]):
        came = swap(balance, "pts", mask)
        balance = balance + (after(came, far_got[0][0]) if mask == masks[-2] else came)
        steps.append(balance)
    for chip in range(chips):
        pair(chip, parts[chips - 1 - chip][-1], steps[-1])
    came = swap(balance, "pts", masks[-1])
    far_got.append(weigh_far(1, steps[-1], list(bounds)))
    balance = balance + after(came, far_got[1][0])
    far_w, far_x = zip(*[(w, x) for w, _, x in far_got])

    bits = powers(half_bit)
    orders = bit_orders(bits)
    cols = width // len(orders)
    m = half_bit // 2
    rows = [*near_x, *far_x]
    total_rows = sum(r.shape[0] for r in rows)
    part = pltpu.VMEM((max(share, LANES), cols), F32)
    def halves(blocks):
        n = len(blocks) // 2
        return [blocks[n:], blocks[:n]] if n else [blocks]

    early, late = [], []
    for r, (_, blocks) in enumerate(orders):
        first, *rest = halves(blocks[m:])
        early.append((r, first))
        late += [(r, blocks) for blocks in rest]
    kept = [(r, blocks[:m]) for r, (_, blocks) in enumerate(orders)]

    def shapes(wanted, dtype):
        return [((len(blocks), share, cols), dtype) for _, blocks in wanted]

    *firsts, assign = call(
        functools.partial(send_kernel, early, half_bit, len(near_w) + len(far_w)),
        shapes(early, BF16) + [((total_rows, slots // 2), BF16)],
        *near_w, *far_w, balance, *rows, scratch=[part],
    )
    got = list(call(
        functools.partial(keep_kernel, late + kept, half_bit), shapes(late, BF16) + shapes(kept, F32),
        assign, *rows, scratch=[part],
    ))
    seconds, keeps = got[: len(late)], got[len(late) :]
    terms = [[k] for k in keeps]
    sends = [[f] + seconds[r : r + 1] for r, f in enumerate(firsts)]
    for step in range(len(bits)):
        for r, (order, _) in enumerate(orders):
            came = [swap(a, "pts", order[step]) for a in sends[r]]
            n = came[0].shape[0]
            if len(came) == 1:
                terms[r].append(came[0])
                continue
            sends[r] = call(
                forward_kernel, [((max(n // 2, 1), share, cols), BF16)] * min(n, 2), keeps[r], came[0], vmem=8
            )
            sends[r] = list(sends[r]) if n > 1 else [sends[r]]
            if n > 1:
                keeps[r] = call(merge_kernel, [((n, share, cols), F32)], keeps[r], came[1], vmem=8)
                terms[r] = [keeps[r]]
            else:
                terms[r].append(came[1])
    flat = [t for route in terms for t in route]
    out = call(
        functools.partial(final_kernel, len(orders), len(terms[0])), [((share, width), BF16)], *flat, base, vmem=8
    )
    return out[None]


def solution(mesh):
    in_specs = (P(("pts", "own"), None), P("pts", None), P(), P(), P("own", None, None))
    out_specs = P("own", "pts", None)
    return jax.shard_map(local, mesh=mesh, in_specs=in_specs, out_specs=out_specs, check_vma=False)
```

```python
import functools

import jax
import jax.numpy as jnp
from jax import lax
from jax.experimental import pallas as pl
from jax.experimental.pallas import tpu as pltpu
from jax.sharding import PartitionSpec as P

F32 = jnp.float32
BF16 = jnp.bfloat16
I32 = jnp.int32
CORES = 2
ROWS = 16
LANES = 128
OWNER_SHIFT = 1 << 17
FIRST_SHIFT = 1 << 7


def down(value):
    return value // ROWS * ROWS


def up(value):
    return -(-value // ROWS) * ROWS


def iota(shape, dim):
    return lax.broadcasted_iota(I32, shape, dim)


def unit_rms(values):
    values = values.astype(F32)
    return values * lax.rsqrt(jnp.mean(values * values, axis=-1, keepdims=True) + 1e-06)


def windows(tok, owners):
    chips = owners // CORES
    full = 2 * tok // owners
    least = CORES * ((tok - full) // max(owners - 1, 1))
    starts = [down(j * least) for j in range(chips)]
    ends = [up(tok - (chips - 1 - j) * least) for j in range(chips)]
    wide = max(e - s for s, e in zip(starts, ends))
    starts = [min(s, tok - wide) for s in starts]
    starts = [min(s, tok - wide) for s in starts]
    soon = starts[min(1, chips - 1)]
    cuts = sorted({0, soon, tok} | {s + wide for s in starts})
    pieces = list(zip(cuts[:-1], cuts[1:]))
    parts = [[k for k, (lo, hi) in enumerate(pieces) if lo < s + wide and s < hi] for s in starts]
    return starts, wide, pieces, parts


def to_col(row):
    n = row.shape[1]
    return jnp.sum(jnp.where(iota((n, n), 0) == iota((n, n), 1), row, 0.0), axis=1, keepdims=True)


def to_row(col):
    n = col.shape[0]
    return jnp.sum(jnp.where(iota((n, n), 0) == iota((n, n), 1), col, 0.0), axis=0, keepdims=True)


def owner_codes(owner_ref, count_ref):
    owner = owner_ref[...].astype(F32)
    count = count_ref[...].astype(F32)
    n = owner.shape[1]
    earlier = (to_col(owner) == owner) & (iota((n, n), 0) < iota((n, n), 1))
    first = jnp.sum(jnp.where(earlier, to_col(count), 0.0), axis=0, keepdims=True)
    return owner * OWNER_SHIFT + first * FIRST_SHIFT + count


def code_and_key(parent_row, code_row, chip, chips):
    parent = to_col(parent_row.astype(F32)).astype(I32)
    tok = parent.shape[0]
    n = code_row.shape[1]
    code = jnp.sum(jnp.where(parent == iota((tok, n), 1), code_row, 0.0), axis=1, keepdims=True)
    owner = code.astype(I32) // OWNER_SHIFT
    order = (chips - 1) - ((owner // CORES) ^ chip)
    key = (order * tok + iota((tok, 1), 0)).astype(F32)
    return code, key


def fetch(pairs, sems):
    copies = [pltpu.make_async_copy(src, dst, sems.at[k]) for k, (src, dst) in enumerate(pairs)]
    for copy in copies:
        copy.start()
    return copies


def sort_kernel(chips, ranges, *refs):
    points_ref, parents_ref, owner_ref, count_ref = refs[:4]
    out_refs, (parents, table, points, owner, count, sems) = refs[4:-6], refs[-6:]
    copies = fetch(
        [(points_ref, points), (parents_ref, parents), (owner_ref, owner), (count_ref, count)], sems
    )
    me = lax.axis_index("own")
    tok = points.shape[0]
    for copy in copies[1:]:
        copy.wait()
    code_row = owner_codes(owner, count)
    table[...] = code_row
    parent = parents[:, pl.ds(pl.multiple_of(me * tok, tok), tok)]
    code, key = code_and_key(parent, code_row, me // CORES, chips)
    key_row = to_row(key)
    place = jnp.sum(jnp.where(key < key_row, 1.0, 0.0), axis=0, keepdims=True).astype(I32)
    pick = jnp.where(iota((tok, tok), 0) == place, 1.0, 0.0).astype(BF16)
    copies[0].wait()
    unit = unit_rms(points[...]).astype(BF16)
    ordered = jnp.dot(pick, unit, preferred_element_type=F32).astype(BF16)
    for (lo, hi), out_ref in zip(ranges, out_refs):
        out_ref[...] = ordered[lo:hi]


def codes_kernel(chips, starts, tok, wide, parents, table, out_ref):
    me = lax.axis_index("own")
    code_row = table[...]
    total = out_ref.shape[1]
    out = jnp.zeros((1, total), F32)
    for rel in range(total // wide):
        parent = parents[:, pl.ds(pl.multiple_of((me ^ rel) * tok, tok), tok)]
        code, key = code_and_key(parent, code_row, (me ^ rel) // CORES, chips)
        place = jnp.sum(jnp.where(to_row(key) < key, 1.0, 0.0), axis=1, keepdims=True).astype(I32)
        inside = iota((tok, total), 1) - rel * wide
        hit = (inside >= 0) & (inside < wide) & (place == inside + starts[chips - 1 - rel // CORES])
        out = out + jnp.sum(jnp.where(hit, code, 0.0), axis=0, keepdims=True)
    out_ref[...] = out


def cent_kernel(in_ref, out_ref, base_ref):
    out_ref[...] = unit_rms(in_ref[...]).astype(BF16)
    share = base_ref.shape[0]
    base_ref[...] = out_ref[pl.ds(pl.multiple_of(lax.axis_index("pts") * share, share), share), :]


def bounds_kernel(places, slots, codes_ref, low_ref, high_ref):
    me = lax.axis_index("own")
    total = codes_ref.shape[1]
    at = 0
    for place, _, size in places:
        part = slice(at, at + size)
        at += size
        hit = iota((size, total), 1) == iota((size, total), 0) + place
        code = jnp.sum(jnp.where(hit, codes_ref[...], 0.0), axis=1, keepdims=True).astype(I32)
        first = (code % OWNER_SHIFT) // FIRST_SHIFT
        low = jnp.where(code // OWNER_SHIFT == me, first, slots)
        low_ref[part, :] = low
        high_ref[part, :] = low + code % FIRST_SHIFT


def coded_kernel(places, tile, half_bit, *refs):
    codes_ref, cent_ref, low_ref, high_ref = refs[-7], refs[-6], refs[-2], refs[-1]
    bounds_kernel(places, cent_ref.shape[0], codes_ref, low_ref, high_ref)
    weights_kernel(places, tile, half_bit, *refs[:-7], low_ref, high_ref, *refs[-6:-2])


def weights_kernel(places, tile, half_bit, *refs):
    row_refs, (low_ref, high_ref, cent_ref, w_ref, sum_ref, rows_ref) = refs[:-6], refs[-6:]
    slots, width = cent_ref.shape
    at = 0
    for row_ref, (_, skip, size) in zip(row_refs, places):
        rows_ref[at : at + size, :] = row_ref[skip : skip + size, :]
        at += size
    span = w_ref.shape[1]
    base = span_start(half_bit, slots, span)

    def step(i, carry):
        at = pl.multiple_of(i * tile, tile)
        cent = cent_ref[pl.ds(pl.multiple_of(base + at, LANES), tile), :]
        scores = lax.dot_general(rows_ref[...], cent, (((1,), (1,)), ((), ())), preferred_element_type=F32)
        slot = iota(scores.shape, 1) + (base + at)
        live = (slot >= low_ref[...]) & (slot < high_ref[...])
        w = jnp.where(live, jnp.exp(scores * (1.0 / (width * 0.05))), 0.0)
        w_ref[:, pl.ds(at, tile)] = w
        sum_ref[:, pl.ds(at, tile)] = jnp.sum(w, axis=0, keepdims=True)
        return carry

    lax.fori_loop(0, span // tile, step, 0, unroll=True)


def span_start(half_bit, slots, span):
    return (lax.axis_index("pts") // half_bit) % 2 * (slots - span)


def inverse(values):
    return jnp.where(values > 0.0, 1.0 / jnp.where(values > 0.0, values, 1.0), 0.0)


def balance_kernel(n, *refs):
    w_refs, col_ref, out_ref = refs[:n], refs[n], refs[n + 1]
    scale = inverse(col_ref[...])
    total = jnp.zeros_like(scale)
    for w_ref in w_refs:
        rows = w_ref.shape[0]
        for at in range(0, rows, ROWS * 2):
            w = w_ref[at : at + ROWS * 2, :]
            row = jnp.sum(w * scale, axis=1, keepdims=True)
            total = total + jnp.sum(w * inverse(row), axis=0, keepdims=True)
    out_ref[...] = total


def assign_kernel(half_bit, *refs):
    w_refs, (t_ref, assign_ref) = refs[:-2], refs[-2:]
    slots, half = t_ref.shape[1], assign_ref.shape[1]
    upper = (lax.axis_index("pts") // half_bit) % 2
    part = inverse(t_ref[:, pl.ds(pl.multiple_of(upper * half, half), half)])
    at = 0
    for w_ref in w_refs:
        span = w_ref.shape[1]
        base = span_start(half_bit, slots, span)
        scale = inverse(t_ref[:, pl.ds(pl.multiple_of(base, LANES), span)])
        columns = pl.ds(pl.multiple_of(upper * (span - half), LANES), half)
        for lo in range(0, w_ref.shape[0], ROWS * 2):
            row = inverse(jnp.sum(w_ref[lo : lo + ROWS * 2, :] * scale, axis=1, keepdims=True))
            mine = w_ref[lo : lo + ROWS * 2, columns] * part
            assign_ref[at : at + ROWS * 2, :] = (mine * row).astype(BF16)
            at += ROWS * 2


def move_kernel(wanted, half_bit, assign_ref, row_refs, out_refs, part_ref):
    low = lax.axis_index("pts") % half_bit
    for (which, order), out_ref in zip(wanted, out_refs):
        share, cols = out_ref.shape[1:]
        block = part_ref.shape[0]
        lanes = slice(which * cols, (which + 1) * cols)
        for k, rel in enumerate(order):
            start = (low ^ rel) * share
            columns = pl.ds(pl.multiple_of(start // block * block, block), block)
            moved, at = 0.0, 0
            for r in row_refs:
                a = assign_ref[at : at + r.shape[0], columns]
                moved = moved + lax.dot_general(
                    a, r[:, lanes], (((0,), (0,)), ((), ())), preferred_element_type=F32
                )
                at += r.shape[0]
            if share < block:
                part_ref[...] = moved
                moved = part_ref[pl.ds(pl.multiple_of(start % block, share), share), :]
            out_ref[k] = moved.astype(out_ref.dtype)


def send_kernel(wanted, half_bit, nw, *refs):
    n = len(wanted)
    row_refs, out_refs = refs[nw + 1 : -n - 2], refs[-n - 2 : -2]
    assign_ref, part_ref = refs[-2:]
    assign_kernel(half_bit, *refs[: nw + 1], assign_ref)
    move_kernel(wanted, half_bit, assign_ref, row_refs, out_refs, part_ref)


def keep_kernel(wanted, half_bit, *refs):
    n = len(wanted)
    move_kernel(wanted, half_bit, refs[0], refs[1 : -n - 1], refs[-n - 1 : -1], refs[-1])


def forward_kernel(keep_ref, came_ref, *out_refs):
    n = came_ref.shape[0]
    total = (keep_ref[n:] + came_ref[...].astype(F32)).astype(BF16)
    at = n
    for out_ref in out_refs:
        at -= out_ref.shape[0]
        out_ref[...] = total[at : at + out_ref.shape[0]]


def merge_kernel(keep_ref, came_ref, out_ref):
    out_ref[...] = keep_ref[: came_ref.shape[0]] + came_ref[...].astype(F32)


def final_kernel(nroute, nterm, *refs):
    base_ref, out_ref = refs[nroute * nterm], refs[nroute * nterm + 1]
    parts = []
    for which in range(nroute):
        total = 0.0
        for ref in refs[which * nterm : (which + 1) * nterm]:
            total = total + ref[0].astype(F32)
        parts.append(total)
    moved = jnp.concatenate(parts, axis=1)
    out_ref[...] = unit_rms(base_ref[...].astype(F32) + 8.0 * moved).astype(BF16)


def call(kernel, outs, *args, scratch=(), flops=0, vmem=16, where=pltpu.VMEM):
    shapes = [jax.ShapeDtypeStruct(s, d) for s, d in outs]
    size = sum(a.size * a.dtype.itemsize for a in args) + sum(s.size * s.dtype.itemsize for s in shapes)
    got = pl.pallas_call(
        kernel,
        out_shape=shapes,
        in_specs=[pl.BlockSpec(memory_space=where)] * len(args),
        out_specs=[pl.BlockSpec(memory_space=pltpu.VMEM)] * len(shapes),
        scratch_shapes=list(scratch),
        compiler_params=pltpu.CompilerParams(vmem_limit_bytes=vmem << 20),
        cost_estimate=pl.CostEstimate(flops=flops, bytes_accessed=0, transcendentals=0),
    )(*args)
    return got[0] if len(shapes) == 1 else got


def after(values, gate):
    return lax.optimization_barrier((values, gate))[0]


def swap(values, axis, bit):
    return lax.ppermute(values, axis, [(i, i ^ bit) for i in range(lax.axis_size(axis))])


def powers(end):
    return [1 << k for k in range(end.bit_length() - 1)]


def bit_orders(bits):
    orders = []
    for k in range(len(bits)):
        order = bits[k:] + bits[:k]
        blocks = [0]
        for bit in reversed(order):
            blocks = blocks + [b | bit for b in blocks]
        orders.append((order, blocks))
    return orders


def local(points, parent_of, owner_of, child_count, centroids):
    owners, groups = lax.axis_size("own"), lax.axis_size("pts")
    chips = owners // CORES
    tok, width = points.shape
    slots = centroids.shape[1]
    share = slots // groups
    starts, wide, pieces, parts = windows(tok, owners)
    parents = parent_of.T
    table = [owner_of.reshape(1, -1), child_count.reshape(1, -1)]
    half_bit = groups // 2
    far_mask = half_bit | half_bit >> 1

    ranges = pieces + [(s, s + wide) for s in starts]
    *ordered, parents, codes = call(
        functools.partial(sort_kernel, chips, ranges),
        [((hi - lo, width), BF16) for lo, hi in ranges] + [(parents.shape, I32), (table[0].shape, F32)],
        points, parents, *table,
        scratch=[
            pltpu.VMEM((tok, width), BF16), *[pltpu.VMEM(a.shape, I32) for a in table],
            pltpu.SemaphoreType.DMA((4,)),
        ],
        where=pl.ANY, vmem=62,
    )
    held, whole = ordered[: len(pieces)], ordered[len(pieces) :]

    def place(chip, core, lo, hi):
        start = starts[chips - 1 - chip]
        first, last = max(lo, start), min(hi, start + wide)
        return (chip * CORES + core) * wide + first - start, first - lo, last - first

    def weigh(rows, places, codes, span=slots, bounds=None):
        count = sum(size for _, _, size in places)
        column = pltpu.VMEM((count, 1), I32)
        return call(
            functools.partial(weights_kernel if bounds else coded_kernel, places, 256 if span % 256 == 0 else span, half_bit),
            [((count, span), F32), ((1, span), F32), ((count, width), BF16)],
            *rows, *(bounds or [codes]), cent, scratch=[] if bounds else [column, column],
        )

    near = [whole[-1]] + [swap(whole[chips - 1 - chip], "own", chip * CORES) for chip in range(1, chips)]
    far_held = [swap(held[0], "pts", far_mask)]
    codes = call(
        functools.partial(codes_kernel, chips, starts, tok, wide), [((1, owners * wide), F32)], parents, codes,
        vmem=4,
    )
    cent, base = call(cent_kernel, [((slots, width), BF16), ((share, width), BF16)], centroids[0])

    far_codes = swap(codes, "pts", far_mask)

    def weigh_near(chip, rows, codes):
        start = starts[chips - 1 - chip]
        return weigh((rows, swap(rows, "own", 1)), [place(chip, c, start, start + wide) for c in range(CORES)], codes)

    near_got = [weigh_near(0, near[0], codes)]
    first = near_got[0][1]
    for chip in range(1, chips):
        near_got.append(weigh_near(chip, after(near[chip], (first, far_held[0], far_codes)), codes))
    near_w, near_s, near_x = zip(*near_got)

    def forward(k, gate):
        for chip in range(1, chips):
            if k in parts[chips - 1 - chip]:
                far_cross[chip, k] = swap(after(far_held[k], gate), "own", chip * CORES)

    def pair(chip, k, gate):
        rows = after(far_cross[chip, k] if chip else far_held[k], gate)
        for core, r in enumerate((rows, swap(rows, "own", 1))):
            far[int(k == parts[chips - 1 - chip][-1])].append((r, place(chip, core, *pieces[k])))

    def weigh_far(late, gate, bounds=None):
        rows, places = zip(*far[late])
        return weigh(rows, places, after(far_codes, gate), min(slots // 2 + LANES, slots), bounds)

    far, far_cross = [[], []], {}
    partial = sum(near_s)
    masks = powers(groups)
    far_held.append(swap(after(held[1], first), "pts", far_mask))
    forward(0, first)
    sums = [partial]
    here = [far_cross[c, 0] for c in range(1, chips) if (c, 0) in far_cross]
    for mask in masks[:-1]:
        sums.append(sums[-1] + swap(sums[-1], "pts", mask))
    sums.append(sums[-1] + swap(after(sums[-1], here), "pts", masks[-1]))
    column = sums[-1]
    for piece in held[2:]:
        far_held.append(swap(after(piece, first), "pts", far_mask))
    balance = call(functools.partial(balance_kernel, chips), [((1, slots), F32)], *near_w, column)
    steps = [balance]
    for k in range(1, len(pieces)):
        forward(k, column)
    for chip in range(chips):
        mine = parts[chips - 1 - chip]
        for k in mine[:-1]:
            pair(chip, k, column)
    late = [place(chip, c, *pieces[parts[chips - 1 - chip][-1]]) for chip in range(chips) for c in range(CORES)]
    count = sum(size for _, _, size in late)
    bounds = call(
        functools.partial(bounds_kernel, late, slots), [((count, 1), I32)] * 2, after(far_codes, steps[0]), vmem=4
    )
    far_got = [weigh_far(0, bounds[0])]
    for k, mask in enumerate(masks[:-1]):
        came = swap(balance, "pts", mask)
        balance = balance + (after(came, far_got[0][0]) if mask == masks[-2] else came)
        steps.append(balance)
    for chip in range(chips):
        pair(chip, parts[chips - 1 - chip][-1], steps[-1])
    came = swap(balance, "pts", masks[-1])
    far_got.append(weigh_far(1, steps[-1], list(bounds)))
    balance = balance + after(came, far_got[1][0])
    far_w, far_x = zip(*[(w, x) for w, _, x in far_got])

    bits = powers(half_bit)
    orders = bit_orders(bits)
    cols = width // len(orders)
    m = half_bit // 2
    rows = [*near_x, *far_x]
    total_rows = sum(r.shape[0] for r in rows)
    part = pltpu.VMEM((max(share, LANES), cols), F32)
    def halves(blocks):
        n = len(blocks) // 2
        return [blocks[n:], blocks[:n]] if n else [blocks]

    early, late = [], []
    for r, (_, blocks) in enumerate(orders):
        first, *rest = halves(blocks[m:])
        early.append((r, first))
        late += [(r, blocks) for blocks in rest]
    kept = [(r, blocks[:m]) for r, (_, blocks) in enumerate(orders)]

    def shapes(wanted, dtype):
        return [((len(blocks), share, cols), dtype) for _, blocks in wanted]

    *firsts, assign = call(
        functools.partial(send_kernel, early, half_bit, len(near_w) + len(far_w)),
        shapes(early, BF16) + [((total_rows, slots // 2), BF16)],
        *near_w, *far_w, balance, *rows, scratch=[part],
    )
    got = list(call(
        functools.partial(keep_kernel, late + kept, half_bit), shapes(late, BF16) + shapes(kept, F32),
        assign, *rows, scratch=[part],
    ))
    seconds, keeps = got[: len(late)], got[len(late) :]
    terms = [[k] for k in keeps]
    sends = [[f] + seconds[r : r + 1] for r, f in enumerate(firsts)]
    for step in range(len(bits)):
        for r, (order, _) in enumerate(orders):
            came = [swap(a, "pts", order[step]) for a in sends[r]]
            n = came[0].shape[0]
            if len(came) == 1:
                terms[r].append(came[0])
                continue
            sends[r] = call(
                forward_kernel, [((max(n // 2, 1), share, cols), BF16)] * min(n, 2), keeps[r], came[0], vmem=8
            )
            sends[r] = list(sends[r]) if n > 1 else [sends[r]]
            if n > 1:
                keeps[r] = call(merge_kernel, [((n, share, cols), F32)], keeps[r], came[1], vmem=8)
                terms[r] = [keeps[r]]
            else:
                terms[r].append(came[1])
    flat = [t for route in terms for t in route]
    out = call(
        functools.partial(final_kernel, len(orders), len(terms[0])), [((share, width), BF16)], *flat, base, vmem=8
    )
    return out[None]


def solution(mesh):
    in_specs = (P(("pts", "own"), None), P("pts", None), P(), P(), P("own", None, None))
    out_specs = P("own", "pts", None)
    return jax.shard_map(local, mesh=mesh, in_specs=in_specs, out_specs=out_specs, check_vma=False)
```
